32 devices in a mesh: fsdp: 4 (over z), req: 8 (over y, x, core).
Axes of the slice: x: 2, y: 2, z: 4, core: 2. Of those that a mesh axis runs over, the one named last changes fastest.
Arguments:
- drafts: bfloat16 [8, 16, 2560], P('req'), may hold values from -6 to 6
- x_weight: bfloat16 [2560, 5120], P('req', 'fsdp'), may hold values from -0.125 to 0.125
- z_weight: bfloat16 [2560, 5120], P('req', 'fsdp'), may hold values from -0.125 to 0.125
- bc_weight: bfloat16 [2560, 256], P('req'), may hold values from -0.125 to 0.125
- dt_weight: bfloat16 [2560, 80], P('req', 'fsdp'), may hold values from -0.125 to 0.125
- dt_bias: float32 [80], P('fsdp'), may hold values from -3 to 0
- decay_rate: float32 [80], P('fsdp'), may hold values from 0.01 to 0.5
- conv_x_weight: bfloat16 [4, 5120], P(None, 'fsdp'), may hold values from -3 to 3
- conv_x_bias: bfloat16 [5120], P('fsdp'), may hold values from -2 to 2
- conv_bc_weight: bfloat16 [4, 256], replicated, may hold values from -3 to 3
- conv_bc_bias: bfloat16 [256], replicated, may hold values from -2 to 2
- norm_gain: bfloat16 [5120], P('fsdp'), may hold values from 0.5 to 1.5
- out_weight: bfloat16 [5120, 2560], P('fsdp', 'req'), may hold values from -0.078125 to 0.078125
- conv_x_state: bfloat16 [8, 3, 5120], P('req', None, 'fsdp'), may hold values from -6 to 6
- conv_bc_state: bfloat16 [8, 3, 256], P('req'), may hold values from -6 to 6
- ssm_state: float32 [8, 80, 64, 128], P('req', 'fsdp'), may hold values from -6 to 6
- sink_x: bfloat16 [8, 4, 5120], P('req', None, 'fsdp'), may hold values from -12 to 12
- sink_b: bfloat16 [8, 4, 128], P('req'), may hold values from -6 to 6
- page_x: bfloat16 [80, 256, 5120], P('req', None, 'fsdp'), may hold values from -3 to 3
- page_b: bfloat16 [80, 256, 128], P('req'), may hold values from -6 to 6
- page_decay: float32 [80, 80, 256], P('req', 'fsdp')
- slot_req: int32 [80], P('req'), may hold values from -1 to 7, as said below
- slot_page: int32 [80], P('req'), may hold values from 0 to 15, as said below
- page_count: int32 [8], replicated, may hold values from 1 to 16, as said below
- accepted: int32 [8], P('req'), may hold values from 1 to 16
- owner_row: int32 [8], replicated, may hold values from 0 to 7, each once
Outputs:
- mixed: bfloat16 [8, 16, 2560], P('req', None, 'fsdp')
- new_state: float32 [8, 80, 64, 128], P('req', 'fsdp')
- new_conv_x: bfloat16 [8, 3, 5120], P('req', None, 'fsdp')
- new_conv_bc: bfloat16 [8, 3, 256], P('req')
The draws below stay inside these ranges and needn't reach their ends.
Inputs may be any that keep to these rules, and one draw needn't show every extreme that they name: `page_count`: one request has 16 pages. `slot_req`: -1 marks an empty slot. Each page 0 to page_count - 1 of every request stands in exactly one slot; a request with fewer than 16 pages also has its page numbered page_count in one slot. `slot_page`: 0 in empty slots. `owner_row`: each row once.
All inputs are finite; a program needn't handle non-finite values.
Results may differ from the reference program's by a relative error of at most 0.015.
Values may be sent and summed in bfloat16 or wider, within the bound.
No kernel may reach another device: no remote copies, remote signals or barrier semaphores. Data moves between devices by JAX's collectives and lax.ppermute only.
A program may use at most 64 MiB of HBM per device.

```python
import math
import jax
import jax.numpy as jnp
from jax import lax

D = 2560
ATTENDER_COUNT = 80
HD = 64
NS = 128
KC = 4
E = 5120
DRAFT = 16
PAGE = 256
WPAGES = 16
SINKS = 4
QUERY_SEQ_COUNT = 8
SLOTS = 80


def page_layout(key):
    count_key, largest_key, layout_random_start = jax.random.split(jax.random.fold_in(key, 11), 3)
    shifts = jax.random.randint(count_key, (QUERY_SEQ_COUNT,), 1, 5).astype(jnp.int32)
    counts = jnp.maximum(jnp.right_shift(jnp.full((QUERY_SEQ_COUNT,), WPAGES, jnp.int32), shifts), 1)
    largest = jax.random.randint(largest_key, (), 0, QUERY_SEQ_COUNT)
    counts = jnp.where(jnp.arange(QUERY_SEQ_COUNT) == largest, WPAGES, counts).astype(jnp.int32)
    placed = counts + (counts < WPAGES).astype(jnp.int32)
    range_ends = jnp.cumsum(placed)
    starts = range_ends - placed
    slot_order = jnp.arange(SLOTS, dtype=jnp.int32)
    request_of = jnp.sum((slot_order[:, None] >= range_ends[None, :]).astype(jnp.int32), axis=1)
    in_use = slot_order < range_ends[-1]
    clipped = jnp.minimum(request_of, QUERY_SEQ_COUNT - 1)
    page_index = slot_order - starts[clipped]
    req_value = jnp.where(in_use, clipped, -1).astype(jnp.int32)
    page_value = jnp.where(in_use, page_index, 0).astype(jnp.int32)
    shuffle = jax.random.permutation(layout_random_start, SLOTS)
    slot_req = jnp.zeros((SLOTS,), jnp.int32).at[shuffle].set(req_value)
    slot_page = jnp.zeros((SLOTS,), jnp.int32).at[shuffle].set(page_value)
    return (counts, slot_req, slot_page)


def draw_page_count(key, part):
    return page_layout(key)[0]


def draw_slot_req(key, part):
    return page_layout(key)[1]


def draw_slot_page(key, part):
    return page_layout(key)[2]


def draw_page_decay(key, part):
    counts, slot_req, slot_page = page_layout(key)
    kind_key, slow_key, fast_key, layout_random_start, extent_random_start = jax.random.split(jax.random.fold_in(key, 23), 5)
    span_extent = WPAGES * PAGE
    fast_pick = jax.random.randint(kind_key, (QUERY_SEQ_COUNT, ATTENDER_COUNT), 0, 2) == 1
    slow_rate = jnp.exp(jax.random.uniform(slow_key, (QUERY_SEQ_COUNT, ATTENDER_COUNT), jnp.float32, math.log(0.05 / span_extent), math.log(2.0 / span_extent)))
    fast_rate = jax.random.uniform(fast_key, (QUERY_SEQ_COUNT, ATTENDER_COUNT), jnp.float32, 1.0 / 50.0, 1.0 / 30.0)
    forgetting_factors = jnp.where(fast_pick, fast_rate, slow_rate)
    spurt_location = jax.random.randint(layout_random_start, (QUERY_SEQ_COUNT, ATTENDER_COUNT, 3), 0, span_extent)
    spurt_extent = jax.random.uniform(extent_random_start, (QUERY_SEQ_COUNT, ATTENDER_COUNT, 3), jnp.float32, 0.22, 0.69)
    guarded_query_index = jnp.maximum(slot_req, 0)
    symbol_separation = (counts[guarded_query_index] - 1 - slot_page)[:, None] * PAGE + (PAGE - 1 - jnp.arange(PAGE))[None, :]
    symbol_separation = jnp.abs(symbol_separation)
    elapsed_symbols = (symbol_separation[:, None, :, None] > spurt_location[guarded_query_index][:, :, None, :]).astype(jnp.float32)
    spurt_clusters = jnp.sum(elapsed_symbols * spurt_extent[guarded_query_index][:, :, None, :], axis=-1)
    return forgetting_factors[guarded_query_index][:, :, None] * symbol_separation[:, None, :].astype(jnp.float32) + spurt_clusters


def touch_ends(values, stream_key, least, top_value):
    place = [jax.random.randint(jax.random.fold_in(stream_key, axis), (), 0, length) for axis, length in enumerate(values.shape)]
    main_axis = values.shape.index(max(values.shape))
    next_to = place[:main_axis] + [(place[main_axis] + 1) % values.shape[main_axis]] + place[main_axis + 1:]
    return values.at[tuple(place)].set(least).at[tuple(next_to)].set(top_value)


def levels(own_key, dims, cuts, low, high):
    def one(position, blocks):
        steps = jax.random.uniform(jax.random.fold_in(jax.random.fold_in(own_key, 6), position), (blocks,), jnp.float32, low / len(cuts), high / len(cuts))
        return jnp.repeat(jnp.exp(steps), dims[position] // blocks).reshape((-1,) + (1,) * (len(dims) - position - 1))

    level = one(*cuts[0])
    for cut in cuts[1:]:
        level = level * one(*cut)
    return level


def noise(key, shape, width, bound, cuts=(), held_as=jnp.bfloat16):
    level = levels(key, shape, cuts, -0.22, 0.18) if cuts else 1.0
    array = jax.random.normal(key, shape, jnp.float32) * width * level
    return jnp.minimum(jnp.maximum(array, -bound), bound).astype(held_as)


def setup_inputs(seed: int = 0) -> dict:
    seeds = jax.random.split(jax.random.key(seed), 27)
    return {
        "drafts": noise(seeds[0], (QUERY_SEQ_COUNT, DRAFT, D), 1.0, 6.0, ((0, 8),)),
        "x_weight": noise(seeds[1], (D, E), D ** -0.5, 0.125, ((0, 8), (1, 4))),
        "z_weight": noise(seeds[2], (D, E), D ** -0.5, 0.125, ((0, 8), (1, 4))),
        "bc_weight": noise(seeds[3], (D, 2 * NS), D ** -0.5, 0.125, ((0, 8),)),
        "dt_weight": noise(seeds[4], (D, ATTENDER_COUNT), D ** -0.5, 0.125, ((0, 8), (1, 4))),
        "dt_bias": jnp.clip(-3.0 + 3.0 * jax.random.uniform(seeds[5], (ATTENDER_COUNT,), jnp.float32) ** levels(seeds[5], (ATTENDER_COUNT,), ((0, 4),), -0.2, 0.2), -3.0, 0.0),
        "decay_rate": jnp.clip(jnp.exp(math.log(0.5) - 3.912023 * jax.random.uniform(seeds[6], (ATTENDER_COUNT,), jnp.float32) ** levels(seeds[6], (ATTENDER_COUNT,), ((0, 4),), -0.2, 0.2)), 0.01, 0.5),
        "conv_x_weight": noise(seeds[7], (KC, E), 0.5, 3.0, ((1, 4),)),
        "conv_x_bias": noise(seeds[8], (E,), 0.3, 2.0, ((0, 4),)),
        "conv_bc_weight": noise(seeds[9], (KC, 2 * NS), 0.5, 3.0),
        "conv_bc_bias": noise(seeds[10], (2 * NS,), 0.3, 2.0),
        "norm_gain": jnp.clip(1.0 + 0.1 * jax.random.normal(seeds[11], (E,), jnp.float32), 0.5, 1.5).astype(jnp.bfloat16),
        "out_weight": noise(seeds[12], (E, D), E ** -0.5, 0.078125, ((0, 4), (1, 8))),
        "conv_x_state": noise(seeds[13], (QUERY_SEQ_COUNT, KC - 1, E), 1.0, 6.0, ((0, 8), (2, 4))),
        "conv_bc_state": noise(seeds[14], (QUERY_SEQ_COUNT, KC - 1, 2 * NS), 1.0, 6.0, ((0, 8),)),
        "ssm_state": noise(seeds[15], (QUERY_SEQ_COUNT, ATTENDER_COUNT, HD, NS), 1.0, 6.0, ((0, 8), (1, 4)), jnp.float32),
        "sink_x": noise(seeds[16], (QUERY_SEQ_COUNT, SINKS, E), 2.0, 12.0, ((0, 8), (2, 4))),
        "sink_b": noise(seeds[17], (QUERY_SEQ_COUNT, SINKS, NS), 1.0, 6.0, ((0, 8),)),
        "page_x": noise(seeds[18], (SLOTS, PAGE, E), 0.5, 3.0, ((0, 8), (2, 4))),
        "page_b": noise(seeds[19], (SLOTS, PAGE, NS), 1.0, 6.0, ((0, 8),)),
        "page_decay": draw_page_decay(jax.random.fold_in(seeds[26], 71), 0),
        "slot_req": draw_slot_req(jax.random.fold_in(seeds[26], 71), 0),
        "slot_page": draw_slot_page(jax.random.fold_in(seeds[26], 71), 0),
        "page_count": draw_page_count(jax.random.fold_in(seeds[26], 71), 0),
        "accepted": touch_ends(jax.random.randint(seeds[24], (QUERY_SEQ_COUNT,), 1, DRAFT + 1), jax.random.fold_in(seeds[24], 1), 1, DRAFT).astype(jnp.int32),
        "owner_row": jax.random.permutation(seeds[25], QUERY_SEQ_COUNT).astype(jnp.int32),
    }


EPSILON = 1e-05

def conv_silu(history, fresh, kernel, offset):
    joined = jnp.concatenate([history, fresh], axis=1).astype(jnp.float32)
    length = fresh.shape[1]
    summed = offset.astype(jnp.float32) + jnp.zeros(fresh.shape, jnp.float32)
    for kernel_tap in range(KC):
        summed = summed + kernel[kernel_tap].astype(jnp.float32) * joined[:, kernel_tap:kernel_tap + length]
    return jax.nn.silu(summed).astype(jnp.bfloat16)

def rounded(values):
    return lax.optimization_barrier(values.astype(jnp.bfloat16)).astype(jnp.float32)

def reference(drafts, x_weight, z_weight, bc_weight, dt_weight, dt_bias, decay_rate, conv_x_weight, conv_x_bias, conv_bc_weight, conv_bc_bias, norm_gain, out_weight, conv_x_state, conv_bc_state, ssm_state, sink_x, sink_b, page_x, page_b, page_decay, slot_req, slot_page, page_count, accepted, owner_row):
    flat_tokens = drafts.reshape(QUERY_SEQ_COUNT * DRAFT, D)
    x_raw = jnp.dot(flat_tokens, x_weight, preferred_element_type=jnp.float32).astype(jnp.bfloat16).reshape(QUERY_SEQ_COUNT, DRAFT, E)
    z_raw = jnp.dot(flat_tokens, z_weight, preferred_element_type=jnp.float32).astype(jnp.bfloat16).reshape(QUERY_SEQ_COUNT, DRAFT, E)
    bc_raw = jnp.dot(flat_tokens, bc_weight, preferred_element_type=jnp.float32).astype(jnp.bfloat16).reshape(QUERY_SEQ_COUNT, DRAFT, 2 * NS)
    dt_raw = jnp.dot(flat_tokens, dt_weight, preferred_element_type=jnp.float32).reshape(QUERY_SEQ_COUNT, DRAFT, ATTENDER_COUNT)
    x_act = conv_silu(conv_x_state, x_raw, conv_x_weight, conv_x_bias)
    bc_act = conv_silu(conv_bc_state, bc_raw, conv_bc_weight, conv_bc_bias)
    b_mat = bc_act[:, :, :NS]
    c_mat = bc_act[:, :, NS:]
    dtime = jax.nn.softplus(dt_raw + dt_bias)
    cumul = jnp.cumsum(-decay_rate * dtime, axis=1)
    guarded_query_index = jnp.maximum(slot_req, 0)
    slot_live = (slot_req >= 0) & (slot_page < page_count[guarded_query_index])
    slot_rows = owner_row[guarded_query_index].astype(jnp.int32)

    def visit(carry, items):
        row_id, alive, values, keys_b, decay_k = items
        scores = jnp.dot(c_mat[row_id], keys_b.T, preferred_element_type=jnp.float32)
        weights = scores[None] * jnp.exp(cumul[row_id].T[:, :, None] - decay_k[:, None, :])
        term = jnp.einsum('htp,phd->thd', rounded(weights), values.reshape(PAGE, ATTENDER_COUNT, HD).astype(jnp.float32))
        term = jnp.where(alive, term, 0.0).reshape(DRAFT, E)
        return (carry.at[row_id].add(term), None)
    page_sum = lax.scan(visit, jnp.zeros((QUERY_SEQ_COUNT, DRAFT, E), jnp.float32), (slot_rows, slot_live, page_x, page_b, page_decay))[0]
    inner = jnp.einsum('rtn,run->rtu', c_mat.astype(jnp.float32), b_mat.astype(jnp.float32))
    later = jnp.arange(DRAFT)[:, None] >= jnp.arange(DRAFT)[None, :]
    spread = jnp.where(later[None, :, :, None], cumul[:, :, None, :] - cumul[:, None, :, :], 0.0)
    draft_weight = jnp.where(later[None, :, :, None], inner[..., None] * jnp.exp(spread) * dtime[:, None, :, :], 0.0)
    head_values = x_act.reshape(QUERY_SEQ_COUNT, DRAFT, ATTENDER_COUNT, HD).astype(jnp.float32)
    own_terms = jnp.einsum('rtuh,ruhp->rthp', rounded(draft_weight), head_values).reshape(QUERY_SEQ_COUNT, DRAFT, E)
    sink_weight = jnp.einsum('rtn,rsn->rts', c_mat.astype(jnp.float32), sink_b.astype(jnp.float32))
    sink_terms = jnp.einsum('rts,rse->rte', rounded(sink_weight), sink_x.astype(jnp.float32))
    mixer_out = page_sum + own_terms + sink_terms
    gated = mixer_out * jax.nn.silu(z_raw.astype(jnp.float32))
    square_mean = lax.optimization_barrier(jnp.sum(gated * gated, axis=-1)) / E
    normed = (gated * lax.rsqrt(square_mean + EPSILON)[..., None] * norm_gain.astype(jnp.float32)).astype(jnp.bfloat16)
    mixed = jnp.dot(normed.reshape(QUERY_SEQ_COUNT * DRAFT, E), out_weight, preferred_element_type=jnp.float32).astype(jnp.bfloat16).reshape(QUERY_SEQ_COUNT, DRAFT, D)
    positions = jnp.arange(DRAFT)
    chosen = positions[None, :] == accepted[:, None] - 1
    cumul_last = lax.optimization_barrier(jnp.sum(jnp.where(chosen[:, :, None], cumul, 0.0), axis=1))
    kept = positions[None, :] < accepted[:, None]
    state_spread = jnp.where(kept[:, :, None], cumul_last[:, None, :] - cumul, 0.0)
    coeff = jnp.where(kept[:, :, None], jnp.exp(state_spread) * dtime, 0.0)
    fresh_state = jnp.einsum('ruh,ruhp,run->rhpn', coeff, head_values, b_mat.astype(jnp.float32), precision=lax.Precision.HIGHEST)
    new_state = jnp.exp(cumul_last)[:, :, None, None] * ssm_state + fresh_state

    def tail_rows(history, fresh_rows):
        joined = jnp.concatenate([history, fresh_rows], axis=1)
        return jax.vmap(lambda seq_rows, first_pos: lax.dynamic_slice_in_dim(seq_rows, first_pos, KC - 1, 0))(joined, accepted.astype(jnp.int32))
    new_conv_x = tail_rows(conv_x_state, x_raw)
    new_conv_bc = tail_rows(conv_bc_state, bc_raw)
    return (mixed, new_state, new_conv_x, new_conv_bc)
```

```python
import functools

import jax
import jax.numpy as jnp
from jax import lax
from jax.experimental import pallas as pl
from jax.experimental.pallas import tpu as pltpu
from jax.sharding import PartitionSpec as P

HD = 64
NS = 128
KC = 4
EPSILON = 1e-05
BF = jnp.bfloat16
F32 = jnp.float32
VMEM_LIMIT = 40 * 1024 * 1024
BCW = 3 * NS


def vmem():
    return pl.BlockSpec(memory_space=pltpu.VMEM)


def smem():
    return pl.BlockSpec(memory_space=pltpu.SMEM)


def call(body, out_shape, in_specs, *args, flops=0, nbytes=0, scratch=()):
    return pl.pallas_call(
        body,
        out_shape=out_shape,
        in_specs=in_specs,
        out_specs=jax.tree.map(lambda _: vmem(), out_shape),
        scratch_shapes=list(scratch),
        compiler_params=pltpu.CompilerParams(vmem_limit_bytes=VMEM_LIMIT),
        cost_estimate=pl.CostEstimate(flops=flops, bytes_accessed=nbytes, transcendentals=0),
    )(*args)


def sds(shape, dtype):
    return jax.ShapeDtypeStruct(shape, dtype)


def silu(v):
    return v / (1.0 + jnp.exp(-v))


def softplus(v):
    return jnp.maximum(v, 0.0) + jnp.log1p(jnp.exp(-jnp.abs(v)))


def conv(history, fresh, taps, offset):
    length = fresh.shape[0]
    joined = jnp.concatenate([history, fresh], axis=0)
    total = offset + taps[0:1] * joined[0:length]
    for k in range(1, KC):
        total = total + taps[k : k + 1] * joined[k : k + length]
    return silu(total)


def running_sum(v):
    length = v.shape[0]
    step = 1
    while step < length:
        v = v + jnp.concatenate([jnp.zeros((step, v.shape[1]), v.dtype), v[: length - step]], axis=0)
        step *= 2
    return v


def head_diag(weights, values):
    heads = len(weights)
    length = weights[0].shape[0]
    if heads == 1:
        return jnp.dot(weights[0], values, preferred_element_type=F32)
    full = jnp.dot(jnp.concatenate(weights, axis=0), values, preferred_element_type=F32)
    owner = lax.broadcasted_iota(jnp.int32, (length, heads * HD), 1) // HD
    out = jnp.where(owner == 0, full[:length], 0.0)
    for i in range(1, heads):
        out = jnp.where(owner == i, full[i * length : (i + 1) * length], out)
    return out


def project_kernel(length, fan, scalar, *refs):
    blocks = refs[:fan]
    xo, xp, zo, zp, bo, bp, do, dp = refs[fan : fan + 8]
    outs = refs[fan + 8 :]
    half = xo.shape[0]
    inner = xo.shape[1]
    heads = do.shape[1]
    tokens = jnp.concatenate([b[0:length, : 2 * half] for b in blocks], axis=0)
    first = scalar[0] == 0
    low, high = tokens[:, :half], tokens[:, half:]
    own = jnp.where(first, low, high)
    other = jnp.where(first, high, low)

    def proj(wo, wp):
        return jnp.dot(own, wo[...], preferred_element_type=F32) + jnp.dot(
            other, wp[...], preferred_element_type=F32
        )

    bc = proj(bo, bp).astype(BF)
    dt = proj(do, dp)
    dt_hi = dt.astype(BF)
    dt_lo = (dt - dt_hi.astype(F32)).astype(BF)
    tail = jnp.concatenate(
        [bc, dt_hi, dt_lo, jnp.zeros((fan * length, NS - 2 * heads), BF)], axis=1
    )
    x = proj(xo, xp).astype(BF)
    z = proj(zo, zp).astype(BF)
    for s, out in enumerate(outs):
        rows = slice(s * length, (s + 1) * length)
        out[:, :inner] = x[rows]
        out[:, inner : 2 * inner] = z[rows]
        for t in range(fan):
            base = 2 * inner + BCW * t
            out[:, base : base + BCW] = tail[t * length : (t + 1) * length]


def mix_kernel(
    length, fan, inner, heads, *refs
):
    parts = refs[:fan]
    blocks = refs[fan : 2 * fan]
    (xs, xw, xb, bw, bb, dt_bias, rate) = refs[2 * fan : 2 * fan + 7]
    packed, x_raw_o, z_raw_o, x_act_o, bc_raw_o, bc_act_o, dtime_o = refs[2 * fan + 7 :]
    bw_f = bw[...].astype(F32)
    bb_f = bb[...].astype(F32)
    for t in range(fan):
        acc = None
        for s in range(fan):
            base = 2 * inner + BCW * ((t + s) % fan)
            piece = parts[s][:, base : base + BCW].astype(F32)
            acc = piece if acc is None else acc + piece
        bc_raw = acc[:, : 2 * NS].astype(BF)
        dt = acc[:, 2 * NS : 2 * NS + heads] + acc[:, 2 * NS + heads : 2 * NS + 2 * heads]
        history = blocks[t][length : 2 * length, : 2 * NS].astype(F32)[: KC - 1]
        bc_act = conv(history, bc_raw.astype(F32), bw_f, bb_f).astype(BF)
        dtime = softplus(dt + dt_bias[...])
        cumul = running_sum(-rate[...] * dtime)
        packed[t * length : (t + 1) * length, :NS] = bc_act[:, NS:].astype(F32)
        packed[t * length : (t + 1) * length, NS:] = jnp.concatenate(
            [cumul, jnp.zeros((length, NS - heads), F32)], axis=1
        )
        if t == 0:
            bc_raw_o[...] = bc_raw
            bc_act_o[...] = bc_act
            dtime_o[...] = dtime
    acc = parts[0][:, : 2 * inner].astype(F32)
    for s in range(1, fan):
        acc = acc + parts[s][:, : 2 * inner].astype(F32)
    x_raw = acc[:, :inner].astype(BF)
    x_raw_o[...] = x_raw
    z_raw_o[...] = acc[:, inner:].astype(BF)
    x_act_o[...] = conv(
        xs[...].astype(F32), x_raw.astype(F32), xw[...].astype(F32), xb[...].astype(F32)
    ).astype(BF)


def page_kernel(
    length, heads, where_ref, live_ref, own_ref, other_ref, b_ref, decay_ref, x_hbm,
    mine_out, other_out, query, total, pages, sems,
):
    slots = x_hbm.shape[0]
    half = own_ref.shape[0]

    def copy(s):
        return pltpu.make_async_copy(x_hbm.at[s], pages.at[s], sems.at[s])

    for s in range(slots):
        @pl.when(live_ref[s] > 0)
        def _():
            copy(s).start()

    query[0:half] = own_ref[...]
    query[half:] = other_ref[...]
    total[...] = jnp.zeros_like(total)

    def visit(s, carry):
        @pl.when(live_ref[s] > 0)
        def _():
            rows = pl.ds(pl.multiple_of(where_ref[s] * length, length), length)
            packed = query[rows, :]
            c_mat = packed[:, :NS].astype(BF)
            cumul = packed[:, NS:]
            scores = lax.dot_general(
                c_mat, b_ref[s], (((1,), (1,)), ((), ())), preferred_element_type=F32
            )
            decay = decay_ref[s]
            copy(s).wait()
            for first in range(0, heads, 4):
                last = min(first + 4, heads)
                weights = [
                    (scores * jnp.exp(cumul[:, h : h + 1] - decay[h : h + 1, :])).astype(BF)
                    for h in range(first, last)
                ]
                cols = slice(first * HD, last * HD)
                total[rows, cols] += head_diag(weights, pages[s, :, cols])
        return carry

    lax.fori_loop(0, slots, visit, 0)
    mine_out[...] = total[0:half].astype(BF)
    other_out[...] = total[half:].astype(BF)


def local_kernel(length, heads, packed, x_act, bc_act, dtime_ref, sink_x, sink_b, out):
    c_mat = bc_act[:, NS:]
    b_mat = bc_act[:, :NS]
    inner = lax.dot_general(c_mat, b_mat, (((1,), (1,)), ((), ())), preferred_element_type=F32)
    cumul = packed[0:length, NS:]
    dtime = jnp.concatenate(
        [dtime_ref[...], jnp.zeros((length, NS - heads), F32)], axis=1
    )
    cumul_t = jnp.transpose(cumul)
    dtime_t = jnp.transpose(dtime)
    row = lax.broadcasted_iota(jnp.int32, (length, length), 0)
    col = lax.broadcasted_iota(jnp.int32, (length, length), 1)
    later = row >= col
    sink_w = lax.dot_general(
        c_mat, sink_b[...], (((1,), (1,)), ((), ())), preferred_element_type=F32
    ).astype(BF).astype(F32)
    for first in range(0, heads, 4):
        last = min(first + 4, heads)
        weights = []
        for h in range(first, last):
            spread = jnp.where(later, cumul[:, h : h + 1] - cumul_t[h : h + 1, :], 0.0)
            weights.append(
                jnp.where(later, inner * jnp.exp(spread) * dtime_t[h : h + 1, :], 0.0).astype(BF)
            )
        cols = slice(first * HD, last * HD)
        acc = head_diag(weights, x_act[:, cols])
        sinks = sink_x[:, cols].astype(F32)
        for q in range(sinks.shape[0]):
            acc = acc + sink_w[:, q : q + 1] * sinks[q : q + 1]
        out[:, cols] = acc


def state_kernel(length, heads, accepted, packed, dtime_ref, x_act, bc_act, ssm, out):
    cumul = packed[0:length, NS : NS + heads]
    count = accepted[0]
    place = lax.broadcasted_iota(jnp.int32, (length, heads), 0)
    last = jnp.sum(jnp.where(place == count - 1, cumul, 0.0), axis=0, keepdims=True)
    kept = place < count
    coeff = jnp.where(kept, jnp.exp(jnp.where(kept, last - cumul, 0.0)) * dtime_ref[...], 0.0)
    factor = jnp.exp(last)
    b_mat = bc_act[:, :NS]
    twice_b = jnp.concatenate([b_mat, b_mat], axis=0)
    for h in range(heads):
        scaled = x_act[:, h * HD : (h + 1) * HD].astype(F32) * coeff[:, h : h + 1]
        high = scaled.astype(BF)
        low = (scaled - high.astype(F32)).astype(BF)
        fresh = lax.dot_general(
            jnp.concatenate([high, low], axis=0), twice_b,
            (((0,), (0,)), ((), ())), preferred_element_type=F32,
        )
        out[h] = factor[:, h : h + 1] * ssm[h] + fresh


def gate_kernel(fan, *refs):
    mine, parts, local, z_raw, out = refs[0], refs[1:fan], refs[fan], refs[fan + 1], refs[fan + 2]
    acc = local[...] + mine[...].astype(F32)
    for p in parts:
        acc = acc + p[...].astype(F32)
    out[...] = (acc * silu(z_raw[...].astype(F32))).astype(BF)


def out_kernel(length, fan, scalar, *refs):
    blocks = refs[:fan]
    gain, wo, wp = refs[fan : fan + 3]
    outs = refs[fan + 3 : 2 * fan + 3]
    whole = refs[2 * fan + 3]
    cols = wo.shape[1]
    g = jnp.concatenate([b[...] for b in blocks], axis=0).astype(F32)
    squares = jnp.sum(g * g, axis=1, keepdims=True)
    scaled = (g * gain[...].astype(F32)).astype(BF)
    own = jnp.dot(scaled, wo[...], preferred_element_type=F32)
    other = jnp.dot(scaled, wp[...], preferred_element_type=F32)
    first = scalar[0] == 0
    high = squares.astype(BF).astype(F32)
    low = squares - high
    lane = lax.broadcasted_iota(jnp.int32, (fan * length, NS), 1)
    whole[:, :cols] = jnp.where(first, own, other)
    whole[:, cols : 2 * cols] = jnp.where(first, other, own)
    whole[:, 2 * cols :] = jnp.where(lane == 0, high, jnp.where(lane == 1, low, 0.0))
    for s, out in enumerate(outs):
        rows = pl.ds(pl.multiple_of(scalar[1 + s] * length, length), length)
        out[...] = whole[rows, :].astype(BF)


def final_kernel(width, inner_total, *refs):
    parts, out = refs[:-1], refs[-1]
    acc = parts[0][...].astype(F32)
    for p in parts[1:]:
        acc = acc + p[...].astype(F32)
    squares = acc[:, width : width + 1] + acc[:, width + 1 : width + 2]
    out[...] = (acc[:, :width] * lax.rsqrt(squares / inner_total + EPSILON)).astype(BF)


def per_device(
    reqs, fan,
    drafts, x_weight, z_weight, bc_weight, dt_weight, dt_bias, decay_rate,
    conv_x_weight, conv_x_bias, conv_bc_weight, conv_bc_bias, norm_gain, out_weight,
    conv_x_state, conv_bc_state, ssm_state, sink_x, sink_b, page_x, page_b, page_decay,
    slot_req, slot_page, page_count, accepted, owner_row,
):
    _, length, width = drafts.shape
    inner = x_weight.shape[1]
    heads = dt_weight.shape[1]
    slots = page_x.shape[0]
    me = lax.axis_index("req")
    zed = lax.axis_index("fsdp")
    pair, side = me // 2, me % 2

    def swap(v):
        return lax.ppermute(v, "req", [(j, j ^ 1) for j in range(reqs)])

    def shift(v, step):
        return lax.ppermute(
            v, "req", [(j, 2 * ((j // 2 + step) % fan) + j % 2) for j in range(reqs)]
        )

    xp, zp, bp, dp = swap(x_weight), swap(z_weight), swap(bc_weight), swap(dt_weight)

    share = width // fan
    wide = max(share, 2 * NS)
    history = jnp.pad(conv_bc_state[0], ((0, length - (KC - 1)), (0, wide - 2 * NS)))

    def draft_block(step):
        start = ((pair + step) % fan) * share
        piece = lax.dynamic_slice(drafts[0], (0, start), (length, share))
        return jnp.concatenate([jnp.pad(piece, ((0, 0), (0, wide - share))), history], axis=0)

    blocks = [draft_block(0)] + [shift(draft_block(s), s) for s in range(1, fan)]

    message = sds((length, 2 * inner + BCW * fan), BF)
    n_cols = 2 * inner + 2 * NS + heads
    parts = call(
        functools.partial(project_kernel, length, fan),
        [message] * fan,
        [smem()] + [vmem()] * (fan + 8),
        side.astype(jnp.int32)[None],
        *blocks, x_weight, xp, z_weight, zp, bc_weight, bp, dt_weight, dp,
        flops=2 * fan * length * share * n_cols, nbytes=2 * share * n_cols,
    )
    parts = [parts[0]] + [shift(parts[s], -s) for s in range(1, fan)]

    packed, x_raw, z_raw, x_act, bc_raw, bc_act, dtime = call(
        functools.partial(mix_kernel, length, fan, inner, heads),
        [
            sds((fan * length, 2 * NS), F32),
            sds((length, inner), BF), sds((length, inner), BF), sds((length, inner), BF),
            sds((length, 2 * NS), BF), sds((length, 2 * NS), BF), sds((length, heads), F32),
        ],
        [vmem()] * (2 * fan + 7),
        *parts, *blocks, conv_x_state[0], conv_x_weight, conv_x_bias[None],
        conv_bc_weight, conv_bc_bias[None], dt_bias[None], decay_rate[None],
        flops=100 * length * inner, nbytes=length * inner * 20,
    )
    packed_other = swap(packed)

    guarded = jnp.maximum(slot_req, 0)
    live = (slot_req >= 0) & (slot_page < page_count[guarded])
    rows = owner_row[guarded]
    where = (rows % 2 != side).astype(jnp.int32) * fan + (pair - rows // 2) % fan
    partial = sds((fan * length, inner), BF)
    mine, others = pl.pallas_call(
        functools.partial(page_kernel, length, heads),
        out_shape=[partial, partial],
        in_specs=[smem(), smem()] + [vmem()] * 4 + [pl.BlockSpec(memory_space=pl.ANY)],
        out_specs=[vmem(), vmem()],
        scratch_shapes=[
            pltpu.VMEM((2 * fan * length, 2 * NS), F32),
            pltpu.VMEM((2 * fan * length, inner), F32),
            pltpu.VMEM(page_x.shape, BF),
            pltpu.SemaphoreType.DMA((slots,)),
        ],
        compiler_params=pltpu.CompilerParams(vmem_limit_bytes=VMEM_LIMIT),
        cost_estimate=pl.CostEstimate(
            flops=8 * slots * length * page_x.shape[1] * inner,
            bytes_accessed=2 * page_x.size, transcendentals=0,
        ),
    )(where.astype(jnp.int32), live.astype(jnp.int32), packed, packed_other, page_b, page_decay, page_x)
    others = swap(others)
    page_parts = (mine.astype(F32) + others.astype(F32)).astype(BF).reshape(fan, length, inner)
    page_parts = [page_parts[0]] + [shift(page_parts[s], -s) for s in range(1, fan)]

    local = call(
        functools.partial(local_kernel, length, heads),
        sds((length, inner), F32), [vmem()] * 6,
        packed, x_act, bc_act, dtime, sink_x[0], sink_b[0],
        flops=40 * length * inner, nbytes=length * inner * 8,
    )
    gated = call(
        functools.partial(gate_kernel, fan),
        sds((length, inner), BF), [vmem()] * (fan + 2),
        *page_parts, local, z_raw,
        flops=40 * length * inner, nbytes=length * inner * 8,
    )

    gated_all = [gated] + [shift(gated, s) for s in range(1, fan)]
    new_state = call(
        functools.partial(state_kernel, length, heads),
        sds(ssm_state.shape[1:], F32), [smem()] + [vmem()] * 5,
        accepted, packed, dtime, x_act, bc_act, ssm_state[0],
        flops=64 * inner * NS, nbytes=8 * inner * NS,
    )

    cols = out_weight.shape[1]
    send = jnp.stack([side] + [(pair - zed - s) % fan for s in range(fan)]).astype(jnp.int32)
    out_shape = sds((length, 2 * cols + NS), BF)
    out_parts = call(
        functools.partial(out_kernel, length, fan),
        [out_shape] * fan,
        [smem()] + [vmem()] * (fan + 3),
        send, *gated_all, norm_gain[None], out_weight, swap(out_weight),
        flops=4 * fan * length * inner * cols, nbytes=4 * inner * cols,
        scratch=[pltpu.VMEM((fan * length, 2 * cols + NS), F32)],
    )

    def to_owner(v, step):
        moves = [
            (f * reqs + j, (j // 2) * reqs + 2 * ((f + step) % fan) + j % 2)
            for f in range(fan)
            for j in range(reqs)
        ]
        return lax.ppermute(v, ("fsdp", "req"), moves)

    arrived = [to_owner(out_parts[s], s) for s in range(fan)]
    mixed = call(
        functools.partial(final_kernel, 2 * cols, inner * fan),
        sds((length, 2 * cols), BF), [vmem()] * fan, *arrived,
        flops=length * cols * 10, nbytes=length * cols * 10,
    )

    def tail_rows(past, fresh):
        joined = jnp.concatenate([past, fresh], axis=0)
        return lax.dynamic_slice_in_dim(joined, accepted[0], KC - 1, 0)[None]

    return (
        mixed[None],
        new_state[None],
        tail_rows(conv_x_state[0], x_raw),
        tail_rows(conv_bc_state[0], bc_raw),
    )


def solution(mesh):
    in_specs = (
        P("req", None, None),
        P("req", "fsdp"),
        P("req", "fsdp"),
        P("req", None),
        P("req", "fsdp"),
        P("fsdp"),
        P("fsdp"),
        P(None, "fsdp"),
        P("fsdp"),
        P(),
        P(),
        P("fsdp"),
        P("fsdp", "req"),
        P("req", None, "fsdp"),
        P("req", None, None),
        P("req", "fsdp", None, None),
        P("req", None, "fsdp"),
        P("req", None, None),
        P("req", None, "fsdp"),
        P("req", None, None),
        P("req", "fsdp", None),
        P("req"),
        P("req"),
        P(),
        P("req"),
        P(),
    )
    out_specs = (
        P("req", None, "fsdp"),
        P("req", "fsdp", None, None),
        P("req", None, "fsdp"),
        P("req", None, None),
    )
    reqs, fan = mesh.shape["req"], mesh.shape["fsdp"]
    assert reqs == 2 * fan
    return jax.shard_map(
        functools.partial(per_device, reqs, fan),
        mesh=mesh, in_specs=in_specs, out_specs=out_specs, check_vma=False,
    )
```

```python
import functools

import jax
import jax.numpy as jnp
from jax import lax
from jax.experimental import pallas as pl
from jax.experimental.pallas import tpu as pltpu
from jax.sharding import PartitionSpec as P

HD = 64
NS = 128
KC = 4
EPSILON = 1e-05
BF = jnp.bfloat16
F32 = jnp.float32
VMEM_LIMIT = 20 * 1024 * 1024
BCW = 3 * NS


def vmem():
    return pl.BlockSpec(memory_space=pltpu.VMEM)


def smem():
    return pl.BlockSpec(memory_space=pltpu.SMEM)


def call(body, out_shape, in_specs, *args, flops=0, nbytes=0, scratch=()):
    return pl.pallas_call(
        body,
        out_shape=out_shape,
        in_specs=in_specs,
        out_specs=jax.tree.map(lambda _: vmem(), out_shape),
        scratch_shapes=list(scratch),
        compiler_params=pltpu.CompilerParams(vmem_limit_bytes=VMEM_LIMIT),
        cost_estimate=pl.CostEstimate(flops=flops, bytes_accessed=nbytes, transcendentals=0),
    )(*args)


def hbm():
    return pl.BlockSpec(memory_space=pltpu.HBM)


def in_hbm(v):
    return pltpu.with_memory_space_constraint(v, pltpu.HBM)


def sds(shape, dtype):
    return jax.ShapeDtypeStruct(shape, dtype)


def silu(v):
    return v / (1.0 + jnp.exp(-v))


def softplus(v):
    return jnp.maximum(v, 0.0) + jnp.log1p(jnp.exp(-jnp.abs(v)))


def conv(history, fresh, taps, offset):
    length = fresh.shape[0]
    joined = jnp.concatenate([history, fresh], axis=0)
    total = offset + taps[0:1] * joined[0:length]
    for k in range(1, KC):
        total = total + taps[k : k + 1] * joined[k : k + length]
    return silu(total)


def running_sum(v):
    length = v.shape[0]
    step = 1
    while step < length:
        v = v + jnp.concatenate([jnp.zeros((step, v.shape[1]), v.dtype), v[: length - step]], axis=0)
        step *= 2
    return v


def head_diag(weights, values):
    heads = len(weights)
    length = weights[0].shape[0]
    if heads == 1:
        return jnp.dot(weights[0], values, preferred_element_type=F32)
    full = jnp.dot(jnp.concatenate(weights, axis=0), values, preferred_element_type=F32)
    owner = lax.broadcasted_iota(jnp.int32, (length, heads * HD), 1) // HD
    out = jnp.where(owner == 0, full[:length], 0.0)
    for i in range(1, heads):
        out = jnp.where(owner == i, full[i * length : (i + 1) * length], out)
    return out


def draft_kernel(fan, share, drafts_hbm, history_hbm, bc_hbm, dt_hbm, x_hbm, z_hbm, out_hbm, *refs):
    outs, (narrow_out, xz_out, drafts, history, steps, sems) = refs[:fan], refs[fan:]
    half, heads = bc_hbm.shape[0], steps.shape[0]
    copies = [
        pltpu.make_async_copy(source, target, sems.at[i])
        for i, (source, target) in enumerate(
            (
                (drafts_hbm, drafts), (history_hbm, history), (dt_hbm, steps),
                (bc_hbm, narrow_out.at[0:half, 0 : 2 * NS]),
                (x_hbm, xz_out.at[0:half]), (z_hbm, xz_out.at[half : 2 * half]),
                (out_hbm, xz_out.at[2 * half : 3 * half]),
            )
        )
    ]
    for c in copies:
        c.start()
    for out in outs:
        out[...] = jnp.zeros_like(out)
    for c in copies[:4]:
        c.wait()
    narrow_out[half : half + heads, :half] = steps[...]
    length = drafts.shape[1]
    pair = lax.axis_index("req") // 2
    past = history[0].astype(F32)
    past = jnp.concatenate([past, jnp.zeros((length - past.shape[0], past.shape[1]), F32)], axis=0)
    if share % 128:
        width = drafts.shape[2]
        whole = pltpu.roll(drafts[0].astype(F32), width - pair * share, 1)
    for s, out in enumerate(outs):
        if share % 128:
            piece = whole[:, s * share : (s + 1) * share].astype(BF)
        else:
            start = pl.multiple_of(((pair + s) % fan) * share, 128)
            piece = drafts[0, :, pl.ds(start, share)]
        out[0:length, :share] = piece
        out[length : 2 * length, : 2 * NS] = past.astype(BF)
    for c in copies[4:]:
        c.wait()


def stage_kernel(count, *refs):
    outs, sems = refs[-1 - count : -1], refs[-1]
    copies = [pltpu.make_async_copy(refs[i], outs[i], sems.at[i]) for i in range(count)]
    for c in copies:
        c.start()
    for c in copies:
        c.wait()


def stage(arrays, after):
    return call(
        functools.partial(stage_kernel, len(arrays)),
        [sds(v.shape, v.dtype) for v in arrays],
        [hbm()] * len(arrays) + [pl.BlockSpec(memory_space=pl.ANY)],
        *[in_hbm(v) for v in arrays], after,
        flops=0, nbytes=sum(2 * v.size for v in arrays),
        scratch=[pltpu.SemaphoreType.DMA((len(arrays),))],
    )


def own_and_other(length, half, blocks):
    tokens = jnp.concatenate([b[0:length, : 2 * half] for b in blocks], axis=0)
    first = lax.axis_index("req") % 2 == 0
    low, high = tokens[:, :half], tokens[:, half:]
    return jnp.where(first, low, high), jnp.where(first, high, low)


def project_bc_kernel(length, fan, half, heads, *refs):
    blocks = refs[:fan]
    mine, theirs, out = refs[fan:]
    own, other = own_and_other(length, half, blocks)
    bc = jnp.dot(own, mine[:half, : 2 * NS], preferred_element_type=F32) + jnp.dot(
        other, theirs[:half, : 2 * NS], preferred_element_type=F32
    )
    turned = (((1,), (1,)), ((), ()))
    rows = slice(half, half + heads)
    dt = lax.dot_general(
        own, mine[rows, :half], turned, preferred_element_type=F32
    ) + lax.dot_general(other, theirs[rows, :half], turned, preferred_element_type=F32)
    dt_hi = dt.astype(BF)
    dt_lo = (dt - dt_hi.astype(F32)).astype(BF)
    out[...] = jnp.concatenate(
        [bc.astype(BF), dt_hi, dt_lo, jnp.zeros((fan * length, NS - 2 * heads), BF)], axis=1
    )


def project_xz_kernel(length, fan, *refs):
    blocks = refs[:fan]
    mine, theirs = refs[fan : fan + 2]
    outs = refs[fan + 2 :]
    half, inner = mine.shape[0] // 3, mine.shape[1]
    own, other = own_and_other(length, half, blocks)
    for i in range(2):
        rows = slice(i * half, (i + 1) * half)
        v = jnp.dot(own, mine[rows], preferred_element_type=F32) + jnp.dot(
            other, theirs[rows], preferred_element_type=F32
        )
        v = v.astype(BF)
        for s, out in enumerate(outs):
            out[:, i * inner : (i + 1) * inner] = v[s * length : (s + 1) * length]


def mix_bc_kernel(length, fan, heads, *refs):
    parts = refs[:fan]
    blocks = refs[fan : 2 * fan]
    taps_ref, offset_ref, bias_ref, rate_ref = refs[2 * fan : 2 * fan + 4]
    packed, bc_raw_o, bc_act_o, dtime_o = refs[2 * fan + 5 :]
    taps, offset = taps_ref[...].astype(F32), offset_ref[...].astype(F32)[None]
    dt_bias, rate = bias_ref[...][None], rate_ref[...][None]
    for t in range(fan):
        acc = None
        for s in range(fan):
            first = length * ((t + s) % fan)
            piece = parts[s][first : first + length].astype(F32)
            acc = piece if acc is None else acc + piece
        bc_raw = acc[:, : 2 * NS].astype(BF)
        dt = acc[:, 2 * NS : 2 * NS + heads] + acc[:, 2 * NS + heads : 2 * NS + 2 * heads]
        history = blocks[t][length : 2 * length, : 2 * NS].astype(F32)[: KC - 1]
        bc_act = conv(history, bc_raw.astype(F32), taps, offset).astype(BF)
        dtime = softplus(dt + dt_bias)
        cumul = running_sum(-rate * dtime)
        packed[t * length : (t + 1) * length, :NS] = bc_act[:, NS:].astype(F32)
        packed[t * length : (t + 1) * length, NS:] = jnp.concatenate(
            [cumul, jnp.zeros((length, NS - heads), F32)], axis=1
        )
        if t == 0:
            bc_raw_o[...] = bc_raw
            bc_act_o[...] = bc_act
            dtime_o[...] = dtime


def page_kernel(
    length, heads, slot_req, slot_page, page_count, owner_row,
    own_ref, other_ref, b_ref, decay_ref, x_hbm, total,
    query, pages, order, scores_ref, sems,
):
    slots = x_hbm.shape[0]
    half = own_ref.shape[0]
    fan = half // length
    me = lax.axis_index("req")

    def request(s):
        return jnp.maximum(slot_req[s], 0)

    def copy(s):
        return pltpu.make_async_copy(x_hbm.at[s], pages.at[s], sems.at[s])

    def place(s):
        row = owner_row[request(s)]
        away = jnp.where(row % 2 == me % 2, 0, fan)
        return (away + (me // 2 - row // 2 + fan) % fan) * length

    count = jnp.int32(0)
    for s in range(slots):
        live = (slot_req[s] >= 0) & (slot_page[s] < page_count[request(s)])

        @pl.when(live)
        def _():
            copy(s).start()
            order[count] = s

        count = count + live.astype(jnp.int32)

    query[0:half] = own_ref[...]
    query[half:] = other_ref[...]
    total[...] = jnp.zeros_like(total)
    for s in range(slots):
        at = pl.ds(pl.multiple_of(place(s), length), length)
        scores_ref[s] = lax.dot_general(
            query[at, :NS].astype(BF), b_ref[s], (((1,), (1,)), ((), ())),
            preferred_element_type=F32,
        )

    def visit(s):
        rows = pl.ds(pl.multiple_of(place(s), length), length)
        scores = scores_ref[s]
        cumul = query[rows, NS:]
        decay = decay_ref[s]
        terms = []
        for first in range(0, heads, 4):
            last = min(first + 4, heads)
            weights = [
                (scores * jnp.exp(cumul[:, h : h + 1] - decay[h : h + 1, :])).astype(BF)
                for h in range(first, last)
            ]
            terms.append(head_diag(weights, pages[s, :, first * HD : last * HD]))
        return rows, terms

    def add(rows, terms):
        first = 0
        for term in terms:
            cols = slice(first, first + term.shape[1])
            total[rows, cols] += term
            first += term.shape[1]

    def two(i, carry):
        one, other = order[2 * i], order[2 * i + 1]
        copy(one).wait()
        copy(other).wait()
        first, second = visit(one), visit(other)
        add(*first)
        add(*second)
        return carry

    lax.fori_loop(0, count // 2, two, 0)

    @pl.when(count % 2 == 1)
    def _():
        s = order[count - 1]
        copy(s).wait()
        add(*visit(s))


def halve_kernel(total, *refs):
    mine, other = refs[-2:]
    half = mine.shape[0]
    mine[...] = total[0:half].astype(BF)
    other[...] = total[half:].astype(BF)


def join_kernel(length, mine, other, _, *outs):
    for s, out in enumerate(outs):
        rows = slice(s * length, (s + 1) * length)
        out[...] = (mine[rows].astype(F32) + other[rows].astype(F32)).astype(BF)


def local_kernel(length, fan, heads, *refs):
    parts = refs[:fan]
    packed, bc_act, dtime_ref, taps, offset, history, sink_x, sink_b = refs[fan : fan + 8]
    out, x_raw_o, x_act_o, silu_z_o = refs[fan + 8 :]
    inner_cols = out.shape[1]
    acc = parts[0][...].astype(F32)
    for s in range(1, fan):
        acc = acc + parts[s][...].astype(F32)
    x_raw = acc[:, :inner_cols].astype(BF)
    x_raw_o[...] = x_raw
    silu_z_o[...] = silu(acc[:, inner_cols:].astype(BF).astype(F32))
    x_act = conv(
        history[0].astype(F32), x_raw.astype(F32), taps[...].astype(F32),
        offset[...].astype(F32)[None],
    ).astype(BF)
    x_act_o[...] = x_act

    c_mat = bc_act[:, NS:]
    b_mat = bc_act[:, :NS]
    turned = (((1,), (1,)), ((), ()))
    inner = lax.dot_general(c_mat, b_mat, turned, preferred_element_type=F32)
    cumul = packed[0:length, NS:]
    dtime = jnp.concatenate(
        [dtime_ref[...], jnp.zeros((length, NS - heads), F32)], axis=1
    )
    cumul_t = jnp.transpose(cumul)
    dtime_t = jnp.transpose(dtime)
    row = lax.broadcasted_iota(jnp.int32, (length, length), 0)
    col = lax.broadcasted_iota(jnp.int32, (length, length), 1)
    later = row >= col
    sink_values = sink_x[0].astype(F32)
    sink_w = lax.dot_general(
        c_mat, sink_b[0], turned, preferred_element_type=F32
    ).astype(BF).astype(F32)
    for first in range(0, heads, 4):
        last = min(first + 4, heads)
        weights = []
        for h in range(first, last):
            spread = jnp.where(later, cumul[:, h : h + 1] - cumul_t[h : h + 1, :], 0.0)
            weights.append(
                jnp.where(later, inner * jnp.exp(spread) * dtime_t[h : h + 1, :], 0.0).astype(BF)
            )
        cols = slice(first * HD, last * HD)
        acc = head_diag(weights, x_act[:, cols])
        for q in range(sink_values.shape[0]):
            acc = acc + sink_w[:, q : q + 1] * sink_values[q : q + 1, cols]
        out[:, cols] = acc


def state_kernel(length, heads, accepted, packed, dtime_ref, x_act, bc_act, ssm, out):
    cumul = packed[0:length, NS : NS + heads]
    count = accepted[0]
    place = lax.broadcasted_iota(jnp.int32, (length, heads), 0)
    last = jnp.sum(jnp.where(place == count - 1, cumul, 0.0), axis=0, keepdims=True)
    kept = place < count
    coeff = jnp.where(kept, jnp.exp(jnp.where(kept, last - cumul, 0.0)) * dtime_ref[...], 0.0)
    factor = jnp.exp(last)
    b_mat = bc_act[:, :NS]
    twice_b = jnp.concatenate([b_mat, b_mat], axis=0)
    for h in range(heads):
        scaled = x_act[:, h * HD : (h + 1) * HD].astype(F32) * coeff[:, h : h + 1]
        high = scaled.astype(BF)
        low = (scaled - high.astype(F32)).astype(BF)
        fresh = lax.dot_general(
            jnp.concatenate([high, low], axis=0), twice_b,
            (((0,), (0,)), ((), ())), preferred_element_type=F32,
        )
        out[h] = factor[:, h : h + 1] * ssm[h] + fresh


def gate_kernel(fan, *refs):
    parts, local, silu_z, out = refs[:fan], refs[fan], refs[fan + 1], refs[fan + 2]
    acc = local[...]
    for p in parts:
        acc = acc + p[...].astype(F32)
    out[...] = (acc * silu_z[...]).astype(BF)


def out_kernel(length, fan, *refs):
    blocks = refs[:fan]
    gain, mine, theirs = refs[fan : fan + 3]
    outs = refs[fan + 3 : 2 * fan + 3]
    whole = refs[2 * fan + 3]
    cols = mine.shape[0] // 3
    me, zed = lax.axis_index("req"), lax.axis_index("fsdp")
    g = jnp.concatenate([b[...] for b in blocks], axis=0).astype(F32)
    squares = jnp.sum(g * g, axis=1, keepdims=True)
    scaled = (g * gain[...].astype(F32)[None]).astype(BF)
    turned = (((1,), (1,)), ((), ()))
    own = lax.dot_general(scaled, mine[2 * cols :], turned, preferred_element_type=F32)
    other = lax.dot_general(scaled, theirs[2 * cols :], turned, preferred_element_type=F32)
    first = me % 2 == 0
    high = squares.astype(BF).astype(F32)
    low = squares - high
    lane = lax.broadcasted_iota(jnp.int32, (fan * length, NS), 1)
    whole[:, :cols] = jnp.where(first, own, other)
    whole[:, cols : 2 * cols] = jnp.where(first, other, own)
    whole[:, 2 * cols :] = jnp.where(lane == 0, high, jnp.where(lane == 1, low, 0.0))
    for s, out in enumerate(outs):
        block = (me // 2 - zed - s + 2 * fan) % fan
        rows = pl.ds(pl.multiple_of(block * length, length), length)
        out[...] = whole[rows, :].astype(BF)


def final_kernel(width, inner_total, *refs):
    parts, out = refs[:-1], refs[-1]
    acc = parts[0][...].astype(F32)
    for p in parts[1:]:
        acc = acc + p[...].astype(F32)
    squares = acc[:, width : width + 1] + acc[:, width + 1 : width + 2]
    out[...] = (acc[:, :width] * lax.rsqrt(squares / inner_total + EPSILON)).astype(BF)


def per_device(
    reqs, fan,
    drafts, x_weight, z_weight, bc_weight, dt_weight, dt_bias, decay_rate,
    conv_x_weight, conv_x_bias, conv_bc_weight, conv_bc_bias, norm_gain, out_weight,
    conv_x_state, conv_bc_state, ssm_state, sink_x, sink_b, page_x, page_b, page_decay,
    slot_req, slot_page, page_count, accepted, owner_row,
):
    _, length, width = drafts.shape
    inner = x_weight.shape[1]
    heads = dt_weight.shape[1]
    slots = page_x.shape[0]

    def swap(v):
        return lax.ppermute(v, "req", [(j, j ^ 1) for j in range(reqs)])

    def shift(v, step):
        return lax.ppermute(
            v, "req", [(j, 2 * ((j // 2 + step) % fan) + j % 2) for j in range(reqs)]
        )

    share = width // fan
    wide = max(share, 2 * NS)
    dt_turned = dt_weight.T
    half = x_weight.shape[0]
    *blocks, narrow, xz_weight = call(
        functools.partial(draft_kernel, fan, share),
        [sds((2 * length, wide), BF)] * fan
        + [sds((half + 2 * length, max(2 * NS, -(-half // 128) * 128)), BF), sds((3 * half, inner), BF)],
        [hbm()] * 7,
        *[in_hbm(v) for v in (drafts, conv_bc_state, bc_weight, dt_turned, x_weight, z_weight, out_weight.T)],
        flops=10, nbytes=2 * length * width,
        scratch=[
            pltpu.VMEM(drafts.shape, BF), pltpu.VMEM(conv_bc_state.shape, BF),
            pltpu.VMEM(dt_turned.shape, BF), pltpu.SemaphoreType.DMA((7,)),
        ],
    )
    blocks = [blocks[0]] + [shift(blocks[s], s) for s in range(1, fan)]

    xz_other = swap(xz_weight)
    bc_cols = 2 * NS + heads
    bc_part = call(
        functools.partial(project_bc_kernel, length, fan, x_weight.shape[0], heads),
        sds((fan * length, BCW), BF), [vmem()] * (fan + 2),
        *blocks, narrow, swap(narrow),
        flops=2 * fan * length * share * bc_cols, nbytes=2 * share * bc_cols,
    )
    bc_parts = [bc_part] + [shift(bc_part, -s) for s in range(1, fan)]
    (
        bc_taps, bc_offset, step_bias, rate,
        x_taps, x_offset, gain, x_past, sinks_x, sinks_b, page_b_here, page_decay_here, *lists,
    ) = stage(
        (
            conv_bc_weight, conv_bc_bias, dt_bias,
            decay_rate, conv_x_weight, conv_x_bias, norm_gain, conv_x_state, sink_x, sink_b,
            page_b, page_decay, slot_req, slot_page, page_count, owner_row,
        ),
        bc_part,
    )
    xz_parts = call(
        functools.partial(project_xz_kernel, length, fan),
        [sds((length, 2 * inner), BF)] * fan,
        [vmem()] * (fan + 2),
        *blocks, xz_weight, xz_other,
        flops=4 * fan * length * share * inner, nbytes=4 * share * inner,
    )
    xz_parts = [xz_parts[0]] + [shift(xz_parts[s], -s) for s in range(1, fan)]
    packed, bc_raw, bc_act, dtime = call(
        functools.partial(mix_bc_kernel, length, fan, heads),
        [
            sds((fan * length, 2 * NS), F32),
            sds((length, 2 * NS), BF), sds((length, 2 * NS), BF), sds((length, heads), F32),
        ],
        [vmem()] * (2 * fan + 4) + [pl.BlockSpec(memory_space=pl.ANY)],
        *bc_parts, *blocks, bc_taps, bc_offset, step_bias, rate, xz_parts[0],
        flops=100 * length * NS, nbytes=length * NS * 20,
    )
    packed_other = swap(packed)

    total = call(
        functools.partial(page_kernel, length, heads),
        sds((2 * fan * length, inner), F32), [smem()] * 4 + [vmem()] * 4 + [hbm()],
        *lists, packed, packed_other, page_b_here, page_decay_here, in_hbm(page_x),
        flops=8 * slots * length * page_x.shape[1] * inner, nbytes=2 * page_x.size,
        scratch=[
            pltpu.VMEM((2 * fan * length, 2 * NS), F32),
            pltpu.VMEM(page_x.shape, BF),
            pltpu.SMEM((slots,), jnp.int32),
            pltpu.VMEM((slots, length, page_x.shape[1]), F32),
            pltpu.SemaphoreType.DMA((slots,)),
        ],
    )
    mine, others = call(
        halve_kernel, [sds((fan * length, inner), BF)] * 2,
        [vmem()] + [pl.BlockSpec(memory_space=pl.ANY)] * fan, total, *xz_parts,
    )
    others = swap(others)
    local, x_raw, x_act, silu_z = call(
        functools.partial(local_kernel, length, fan, heads),
        [sds((length, inner), F32), sds((length, inner), BF), sds((length, inner), BF), sds((length, inner), F32)],
        [vmem()] * (fan + 8),
        *xz_parts, packed, bc_act, dtime, x_taps, x_offset, x_past, sinks_x, sinks_b,
        flops=40 * length * inner, nbytes=length * inner * 8,
    )
    parts = call(
        functools.partial(join_kernel, length),
        [sds((length, inner), BF)] * fan, [vmem()] * 2 + [pl.BlockSpec(memory_space=pl.ANY)],
        mine, others, local,
        flops=fan * length * inner, nbytes=fan * length * inner * 6,
    )
    parts = [parts[0]] + [shift(parts[s], -s) for s in range(1, fan)]
    gated = call(
        functools.partial(gate_kernel, fan),
        sds((length, inner), BF), [vmem()] * (fan + 2),
        *parts, local, silu_z,
        flops=40 * length * inner, nbytes=length * inner * 8,
    )

    gated_all = [gated] + [shift(gated, s) for s in range(1, fan)]
    new_state = call(
        functools.partial(state_kernel, length, heads),
        sds(ssm_state.shape[1:], F32), [smem()] + [vmem()] * 5,
        accepted, packed, dtime, x_act, bc_act, ssm_state[0],
        flops=64 * inner * NS, nbytes=8 * inner * NS,
    )

    cols = out_weight.shape[1]
    out_shape = sds((length, 2 * cols + NS), BF)
    out_parts = call(
        functools.partial(out_kernel, length, fan),
        [out_shape] * fan, [vmem()] * (fan + 3),
        *gated_all, gain, xz_weight, xz_other,
        flops=4 * fan * length * inner * cols, nbytes=4 * inner * cols,
        scratch=[pltpu.VMEM((fan * length, 2 * cols + NS), F32)],
    )

    def to_owner(v, step):
        moves = [
            (f * reqs + j, (j // 2) * reqs + 2 * ((f + step) % fan) + j % 2)
            for f in range(fan)
            for j in range(reqs)
        ]
        return lax.ppermute(v, ("fsdp", "req"), moves)

    arrived = [to_owner(out_parts[s], s) for s in range(fan)]
    mixed = call(
        functools.partial(final_kernel, 2 * cols, inner * fan),
        sds((length, 2 * cols), BF), [vmem()] * fan, *arrived,
        flops=length * cols * 10, nbytes=length * cols * 10,
    )

    def tail_rows(past, fresh):
        joined = jnp.concatenate([past, fresh], axis=0)
        return lax.dynamic_slice_in_dim(joined, accepted[0], KC - 1, 0)[None]

    return (
        mixed[None],
        new_state[None],
        tail_rows(conv_x_state[0], x_raw),
        tail_rows(conv_bc_state[0], bc_raw),
    )


def solution(mesh):
    in_specs = (
        P("req", None, None),
        P("req", "fsdp"),
        P("req", "fsdp"),
        P("req", None),
        P("req", "fsdp"),
        P("fsdp"),
        P("fsdp"),
        P(None, "fsdp"),
        P("fsdp"),
        P(),
        P(),
        P("fsdp"),
        P("fsdp", "req"),
        P("req", None, "fsdp"),
        P("req", None, None),
        P("req", "fsdp", None, None),
        P("req", None, "fsdp"),
        P("req", None, None),
        P("req", None, "fsdp"),
        P("req", None, None),
        P("req", "fsdp", None),
        P("req"),
        P("req"),
        P(),
        P("req"),
        P(),
    )
    out_specs = (
        P("req", None, "fsdp"),
        P("req", "fsdp", None, None),
        P("req", None, "fsdp"),
        P("req", None, None),
    )
    reqs, fan = mesh.shape["req"], mesh.shape["fsdp"]
    assert reqs == 2 * fan
    return jax.shard_map(
        functools.partial(per_device, reqs, fan),
        mesh=mesh, in_specs=in_specs, out_specs=out_specs, check_vma=False,
    )
```

```python
import functools

import jax
import jax.numpy as jnp
from jax import lax
from jax.experimental import pallas as pl
from jax.experimental.pallas import tpu as pltpu
from jax.sharding import PartitionSpec as P

HD = 64
NS = 128
KC = 4
EPSILON = 1e-05
BF = jnp.bfloat16
F32 = jnp.float32
VMEM_LIMIT = 20 * 1024 * 1024
BCW = 3 * NS


def vmem():
    return pl.BlockSpec(memory_space=pltpu.VMEM)


def smem():
    return pl.BlockSpec(memory_space=pltpu.SMEM)


def call(body, out_shape, in_specs, *args, flops=0, nbytes=0, scratch=()):
    return pl.pallas_call(
        body,
        out_shape=out_shape,
        in_specs=in_specs,
        out_specs=jax.tree.map(lambda _: vmem(), out_shape),
        scratch_shapes=list(scratch),
        compiler_params=pltpu.CompilerParams(vmem_limit_bytes=VMEM_LIMIT),
        cost_estimate=pl.CostEstimate(flops=flops, bytes_accessed=nbytes, transcendentals=0),
    )(*args)


def hbm():
    return pl.BlockSpec(memory_space=pltpu.HBM)


def in_hbm(v):
    return pltpu.with_memory_space_constraint(v, pltpu.HBM)


def sds(shape, dtype):
    return jax.ShapeDtypeStruct(shape, dtype)


def silu(v):
    return v / (1.0 + jnp.exp(-v))


def softplus(v):
    return jnp.maximum(v, 0.0) + jnp.log1p(jnp.exp(-jnp.abs(v)))


def conv(history, fresh, taps, offset):
    length = fresh.shape[0]
    joined = jnp.concatenate([history, fresh], axis=0)
    total = offset + taps[0:1] * joined[0:length]
    for k in range(1, KC):
        total = total + taps[k : k + 1] * joined[k : k + length]
    return silu(total)


def running_sum(v):
    length = v.shape[0]
    step = 1
    while step < length:
        v = v + jnp.concatenate([jnp.zeros((step, v.shape[1]), v.dtype), v[: length - step]], axis=0)
        step *= 2
    return v


def head_diag(weights, values):
    heads = len(weights)
    length = weights[0].shape[0]
    if heads == 1:
        return jnp.dot(weights[0], values, preferred_element_type=F32)
    full = jnp.dot(jnp.concatenate(weights, axis=0), values, preferred_element_type=F32)
    owner = lax.broadcasted_iota(jnp.int32, (length, heads * HD), 1) // HD
    out = jnp.where(owner == 0, full[:length], 0.0)
    for i in range(1, heads):
        out = jnp.where(owner == i, full[i * length : (i + 1) * length], out)
    return out


def draft_kernel(fan, share, drafts_hbm, history_hbm, bc_hbm, dt_hbm, x_hbm, z_hbm, out_hbm, *refs):
    outs, (narrow_out, xz_out, drafts, history, steps, sems) = refs[:fan], refs[fan:]
    half, heads = bc_hbm.shape[0], steps.shape[0]
    copies = [
        pltpu.make_async_copy(source, target, sems.at[i])
        for i, (source, target) in enumerate(
            (
                (drafts_hbm, drafts), (history_hbm, history), (dt_hbm, steps),
                (bc_hbm, narrow_out.at[0:half, 0 : 2 * NS]),
                (x_hbm, xz_out.at[0:half]), (z_hbm, xz_out.at[half : 2 * half]),
                (out_hbm, xz_out.at[2 * half : 3 * half]),
            )
        )
    ]
    for c in copies:
        c.start()
    for out in outs:
        out[...] = jnp.zeros_like(out)
    for c in copies[:4]:
        c.wait()
    narrow_out[half : half + heads, :half] = steps[...]
    length = drafts.shape[1]
    pair = lax.axis_index("req") // 2
    past = history[0].astype(F32)
    past = jnp.concatenate([past, jnp.zeros((length - past.shape[0], past.shape[1]), F32)], axis=0)
    if share % 128:
        width = drafts.shape[2]
        whole = drafts[0].astype(F32)
    for s, out in enumerate(outs):
        if share % 128:
            shift = (width - (pair ^ s) * share) % width
            piece = pltpu.roll(whole, shift, 1)[:, :share].astype(BF)
        else:
            start = pl.multiple_of((pair ^ s) * share, 128)
            piece = drafts[0, :, pl.ds(start, share)]
        out[0:length, :share] = piece
        out[length : 2 * length, : 2 * NS] = past.astype(BF)
    for c in copies[4:]:
        c.wait()


def stage_kernel(count, *refs):
    outs, sems = refs[-1 - count : -1], refs[-1]
    copies = [pltpu.make_async_copy(refs[i], outs[i], sems.at[i]) for i in range(count)]
    for c in copies:
        c.start()
    for c in copies:
        c.wait()


def stage(arrays, after):
    return call(
        functools.partial(stage_kernel, len(arrays)),
        [sds(v.shape, v.dtype) for v in arrays],
        [hbm()] * len(arrays) + [pl.BlockSpec(memory_space=pl.ANY)],
        *[in_hbm(v) for v in arrays], after,
        flops=0, nbytes=sum(2 * v.size for v in arrays),
        scratch=[pltpu.SemaphoreType.DMA((len(arrays),))],
    )


def own_and_other(length, half, blocks):
    tokens = jnp.concatenate([b[0:length, : 2 * half] for b in blocks], axis=0)
    first = lax.axis_index("req") % 2 == 0
    low, high = tokens[:, :half], tokens[:, half:]
    return jnp.where(first, low, high), jnp.where(first, high, low)


def project_bc_kernel(length, fan, half, heads, *refs):
    blocks = refs[:fan]
    mine, theirs, out = refs[fan:]
    own, other = own_and_other(length, half, blocks)
    bc = jnp.dot(own, mine[:half, : 2 * NS], preferred_element_type=F32) + jnp.dot(
        other, theirs[:half, : 2 * NS], preferred_element_type=F32
    )
    turned = (((1,), (1,)), ((), ()))
    rows = slice(half, half + heads)
    dt = lax.dot_general(
        own, mine[rows, :half], turned, preferred_element_type=F32
    ) + lax.dot_general(other, theirs[rows, :half], turned, preferred_element_type=F32)
    dt_hi = dt.astype(BF)
    dt_lo = (dt - dt_hi.astype(F32)).astype(BF)
    out[...] = jnp.concatenate(
        [bc.astype(BF), dt_hi, dt_lo, jnp.zeros((fan * length, NS - 2 * heads), BF)], axis=1
    )


def project_xz_kernel(length, fan, *refs):
    blocks = refs[:fan]
    mine, theirs = refs[fan : fan + 2]
    out, out_pair = refs[fan + 2 :]
    half, inner = mine.shape[0] // 3, mine.shape[1]
    own, other = own_and_other(length, half, blocks)
    for i in range(2):
        rows = slice(i * half, (i + 1) * half)
        v = jnp.dot(own, mine[rows], preferred_element_type=F32) + jnp.dot(
            other, theirs[rows], preferred_element_type=F32
        )
        out[:, i * inner : (i + 1) * inner] = v.astype(BF)
    first = lax.axis_index("req") % 2 == 0
    a, b = mine[2 * half :], theirs[2 * half :]
    out_pair[0:half] = jnp.where(first, a, b)
    out_pair[half:] = jnp.where(first, b, a)


def mix_bc_kernel(length, fan, heads, *refs):
    parts = refs[:fan]
    blocks = refs[fan : 2 * fan]
    taps_ref, offset_ref, bias_ref, rate_ref = refs[2 * fan : 2 * fan + 4]
    packed, bc_raw_o, bc_act_o, dtime_o = refs[2 * fan + 5 :]
    taps, offset = taps_ref[...].astype(F32), offset_ref[...].astype(F32)[None]
    dt_bias, rate = bias_ref[...][None], rate_ref[...][None]
    for t in range(fan):
        acc = None
        for s in range(fan):
            first = length * (t ^ s)
            piece = parts[s][first : first + length].astype(F32)
            acc = piece if acc is None else acc + piece
        bc_raw = acc[:, : 2 * NS].astype(BF)
        dt = acc[:, 2 * NS : 2 * NS + heads] + acc[:, 2 * NS + heads : 2 * NS + 2 * heads]
        history = blocks[t][length : 2 * length, : 2 * NS].astype(F32)[: KC - 1]
        bc_act = conv(history, bc_raw.astype(F32), taps, offset).astype(BF)
        dtime = softplus(dt + dt_bias)
        cumul = running_sum(-rate * dtime)
        packed[t * length : (t + 1) * length, :NS] = bc_act[:, NS:].astype(F32)
        packed[t * length : (t + 1) * length, NS:] = jnp.concatenate(
            [cumul, jnp.zeros((length, NS - heads), F32)], axis=1
        )
        if t == 0:
            bc_raw_o[...] = bc_raw
            bc_act_o[...] = bc_act
            dtime_o[...] = dtime


def page_kernel(
    length, heads, slot_req, slot_page, page_count, owner_row,
    own_ref, other_ref, b_ref, decay_ref, x_hbm, total,
    query, pages, order, scores_ref, sems,
):
    slots = x_hbm.shape[0]
    half = own_ref.shape[0]
    fan = half // length
    me = lax.axis_index("req")

    def request(s):
        return jnp.maximum(slot_req[s], 0)

    def copy(s):
        return pltpu.make_async_copy(x_hbm.at[s], pages.at[s], sems.at[s])

    def place(s):
        row = owner_row[request(s)]
        away = jnp.where(row % 2 == me % 2, 0, fan)
        return (away + (me // 2 ^ row // 2)) * length

    count = jnp.int32(0)
    for s in range(slots):
        live = (slot_req[s] >= 0) & (slot_page[s] < page_count[request(s)])

        @pl.when(live)
        def _():
            copy(s).start()
            order[count] = s

        count = count + live.astype(jnp.int32)

    query[0:half] = own_ref[...]
    query[half:] = other_ref[...]
    total[...] = jnp.zeros_like(total)
    for s in range(slots):
        at = pl.ds(pl.multiple_of(place(s), length), length)
        scores_ref[s] = lax.dot_general(
            query[at, :NS].astype(BF), b_ref[s], (((1,), (1,)), ((), ())),
            preferred_element_type=F32,
        )

    def visit(s):
        rows = pl.ds(pl.multiple_of(place(s), length), length)
        scores = scores_ref[s]
        cumul = query[rows, NS:]
        decay = decay_ref[s]
        terms = []
        for first in range(0, heads, 4):
            last = min(first + 4, heads)
            weights = [
                (scores * jnp.exp(cumul[:, h : h + 1] - decay[h : h + 1, :])).astype(BF)
                for h in range(first, last)
            ]
            terms.append(head_diag(weights, pages[s, :, first * HD : last * HD]))
        return rows, terms

    def add(rows, terms):
        first = 0
        for term in terms:
            cols = slice(first, first + term.shape[1])
            total[rows, cols] += term
            first += term.shape[1]

    def two(i, carry):
        one, other = order[2 * i], order[2 * i + 1]
        copy(one).wait()
        copy(other).wait()
        first, second = visit(one), visit(other)
        add(*first)
        add(*second)
        return carry

    lax.fori_loop(0, count // 2, two, 0)

    @pl.when(count % 2 == 1)
    def _():
        s = order[count - 1]
        copy(s).wait()
        add(*visit(s))


def halve_kernel(total, mine, other):
    half = mine.shape[0]
    mine[...] = total[0:half].astype(BF)
    other[...] = total[half:].astype(BF)


def join_kernel(length, mine, other, xz, *outs):
    inner = mine.shape[1]
    for s, out in enumerate(outs):
        rows = slice(s * length, (s + 1) * length)
        out[:, :inner] = (mine[rows].astype(F32) + other[rows].astype(F32)).astype(BF)
        out[:, inner:] = xz[rows]


def local_kernel(length, fan, heads, *refs):
    parts = refs[:fan]
    packed, bc_act, dtime_ref, taps, offset, history, sink_x, sink_b = refs[fan : fan + 8]
    out, x_raw_o, x_act_o = refs[fan + 8 :]
    inner_cols = out.shape[1]
    acc = parts[0][...].astype(F32)
    for s in range(1, fan):
        acc = acc + parts[s][...].astype(F32)
    page_sum = acc[:, :inner_cols]
    x_raw = acc[:, inner_cols : 2 * inner_cols].astype(BF)
    x_raw_o[...] = x_raw
    silu_z = silu(acc[:, 2 * inner_cols :].astype(BF).astype(F32))
    x_act = conv(
        history[0].astype(F32), x_raw.astype(F32), taps[...].astype(F32),
        offset[...].astype(F32)[None],
    ).astype(BF)
    x_act_o[...] = x_act

    c_mat = bc_act[:, NS:]
    b_mat = bc_act[:, :NS]
    turned = (((1,), (1,)), ((), ()))
    inner = lax.dot_general(c_mat, b_mat, turned, preferred_element_type=F32)
    cumul = packed[0:length, NS:]
    dtime = jnp.concatenate(
        [dtime_ref[...], jnp.zeros((length, NS - heads), F32)], axis=1
    )
    cumul_t = jnp.transpose(cumul)
    dtime_t = jnp.transpose(dtime)
    row = lax.broadcasted_iota(jnp.int32, (length, length), 0)
    col = lax.broadcasted_iota(jnp.int32, (length, length), 1)
    later = row >= col
    sink_values = sink_x[0].astype(F32)
    sink_w = lax.dot_general(
        c_mat, sink_b[0], turned, preferred_element_type=F32
    ).astype(BF).astype(F32)
    for first in range(0, heads, 4):
        last = min(first + 4, heads)
        weights = []
        for h in range(first, last):
            spread = jnp.where(later, cumul[:, h : h + 1] - cumul_t[h : h + 1, :], 0.0)
            weights.append(
                jnp.where(later, inner * jnp.exp(spread) * dtime_t[h : h + 1, :], 0.0).astype(BF)
            )
        cols = slice(first * HD, last * HD)
        acc = page_sum[:, cols] + head_diag(weights, x_act[:, cols])
        for q in range(sink_values.shape[0]):
            acc = acc + sink_w[:, q : q + 1] * sink_values[q : q + 1, cols]
        out[:, cols] = (acc * silu_z[:, cols]).astype(BF)


def state_kernel(length, heads, accepted, packed, dtime_ref, x_act, bc_act, ssm, out):
    cumul = packed[0:length, NS : NS + heads]
    count = accepted[0]
    place = lax.broadcasted_iota(jnp.int32, (length, heads), 0)
    last = jnp.sum(jnp.where(place == count - 1, cumul, 0.0), axis=0, keepdims=True)
    kept = place < count
    coeff = jnp.where(kept, jnp.exp(jnp.where(kept, last - cumul, 0.0)) * dtime_ref[...], 0.0)
    factor = jnp.exp(last)
    b_mat = bc_act[:, :NS]
    twice_b = jnp.concatenate([b_mat, b_mat], axis=0)
    for h in range(heads):
        scaled = x_act[:, h * HD : (h + 1) * HD].astype(F32) * coeff[:, h : h + 1]
        high = scaled.astype(BF)
        low = (scaled - high.astype(F32)).astype(BF)
        fresh = lax.dot_general(
            jnp.concatenate([high, low], axis=0), twice_b,
            (((0,), (0,)), ((), ())), preferred_element_type=F32,
        )
        out[h] = factor[:, h : h + 1] * ssm[h] + fresh


def out_kernel(length, fan, *refs):
    blocks = refs[:fan]
    gain, weights = refs[fan : fan + 2]
    outs = refs[fan + 2 : 2 * fan + 2]
    whole = refs[2 * fan + 2]
    cols = weights.shape[0]
    me, zed = lax.axis_index("req"), lax.axis_index("fsdp")
    g = jnp.concatenate([b[...] for b in blocks], axis=0).astype(F32)
    squares = jnp.sum(g * g, axis=1, keepdims=True)
    scaled = (g * gain[...].astype(F32)[None]).astype(BF)
    high = squares.astype(BF).astype(F32)
    low = squares - high
    lane = lax.broadcasted_iota(jnp.int32, (fan * length, NS), 1)
    whole[:, :cols] = lax.dot_general(
        scaled, weights[...], (((1,), (1,)), ((), ())), preferred_element_type=F32
    )
    whole[:, cols:] = jnp.where(lane == 0, high, jnp.where(lane == 1, low, 0.0))
    for s, out in enumerate(outs):
        block = me // 2 ^ zed ^ s
        rows = pl.ds(pl.multiple_of(block * length, length), length)
        out[...] = whole[rows, :].astype(BF)


def final_kernel(width, inner_total, *refs):
    parts, out = refs[:-1], refs[-1]
    acc = parts[0][...].astype(F32)
    for p in parts[1:]:
        acc = acc + p[...].astype(F32)
    squares = acc[:, width : width + 1] + acc[:, width + 1 : width + 2]
    out[...] = (acc[:, :width] * lax.rsqrt(squares / inner_total + EPSILON)).astype(BF)


def per_device(
    reqs, fan,
    drafts, x_weight, z_weight, bc_weight, dt_weight, dt_bias, decay_rate,
    conv_x_weight, conv_x_bias, conv_bc_weight, conv_bc_bias, norm_gain, out_weight,
    conv_x_state, conv_bc_state, ssm_state, sink_x, sink_b, page_x, page_b, page_decay,
    slot_req, slot_page, page_count, accepted, owner_row,
):
    _, length, width = drafts.shape
    inner = x_weight.shape[1]
    heads = dt_weight.shape[1]
    slots = page_x.shape[0]

    def swap(v):
        return lax.ppermute(v, "req", [(j, j ^ 1) for j in range(reqs)])

    def shift(v, step):
        return lax.ppermute(v, "req", [(j, j ^ 2 * step) for j in range(reqs)])

    share = width // fan
    wide = max(share, 2 * NS)
    dt_turned = dt_weight.T
    half = x_weight.shape[0]
    *blocks, narrow, xz_weight = call(
        functools.partial(draft_kernel, fan, share),
        [sds((2 * length, wide), BF)] * fan
        + [sds((half + 2 * length, max(2 * NS, -(-half // 128) * 128)), BF), sds((3 * half, inner), BF)],
        [hbm()] * 7,
        *[in_hbm(v) for v in (drafts, conv_bc_state, bc_weight, dt_turned, x_weight, z_weight, out_weight.T)],
        flops=10, nbytes=2 * length * width,
        scratch=[
            pltpu.VMEM(drafts.shape, BF), pltpu.VMEM(conv_bc_state.shape, BF),
            pltpu.VMEM(dt_turned.shape, BF), pltpu.SemaphoreType.DMA((7,)),
        ],
    )
    blocks = [blocks[0]] + [shift(blocks[s], s) for s in range(1, fan)]

    xz_other = swap(xz_weight)
    bc_cols = 2 * NS + heads
    bc_part = call(
        functools.partial(project_bc_kernel, length, fan, x_weight.shape[0], heads),
        sds((fan * length, BCW), BF), [vmem()] * (fan + 2),
        *blocks, narrow, swap(narrow),
        flops=2 * fan * length * share * bc_cols, nbytes=2 * share * bc_cols,
    )
    bc_parts = [bc_part] + [shift(bc_part, s) for s in range(1, fan)]
    (
        bc_taps, bc_offset, step_bias, rate,
        x_taps, x_offset, gain, x_past, sinks_x, sinks_b, page_b_here, page_decay_here, *lists,
    ) = stage(
        (
            conv_bc_weight, conv_bc_bias, dt_bias,
            decay_rate, conv_x_weight, conv_x_bias, norm_gain, conv_x_state, sink_x, sink_b,
            page_b, page_decay, slot_req, slot_page, page_count, owner_row,
        ),
        bc_part,
    )
    xz_part, out_pair = call(
        functools.partial(project_xz_kernel, length, fan),
        [sds((fan * length, 2 * inner), BF), sds((2 * half, inner), BF)],
        [vmem()] * (fan + 2),
        *blocks, xz_weight, xz_other,
        flops=4 * fan * length * share * inner, nbytes=4 * share * inner,
    )
    packed, bc_raw, bc_act, dtime = call(
        functools.partial(mix_bc_kernel, length, fan, heads),
        [
            sds((fan * length, 2 * NS), F32),
            sds((length, 2 * NS), BF), sds((length, 2 * NS), BF), sds((length, heads), F32),
        ],
        [vmem()] * (2 * fan + 4) + [pl.BlockSpec(memory_space=pl.ANY)],
        *bc_parts, *blocks, bc_taps, bc_offset, step_bias, rate, xz_part,
        flops=100 * length * NS, nbytes=length * NS * 20,
    )
    packed_other = swap(packed)

    total = call(
        functools.partial(page_kernel, length, heads),
        sds((2 * fan * length, inner), F32), [smem()] * 4 + [vmem()] * 4 + [hbm()],
        *lists, packed, packed_other, page_b_here, page_decay_here, in_hbm(page_x),
        flops=8 * slots * length * page_x.shape[1] * inner, nbytes=2 * page_x.size,
        scratch=[
            pltpu.VMEM((2 * fan * length, 2 * NS), F32),
            pltpu.VMEM(page_x.shape, BF),
            pltpu.SMEM((slots,), jnp.int32),
            pltpu.VMEM((slots, length, page_x.shape[1]), F32),
            pltpu.SemaphoreType.DMA((slots,)),
        ],
    )
    mine, others = call(
        halve_kernel, [sds((fan * length, inner), BF)] * 2,
        [vmem()], total,
    )
    others = swap(others)
    parts = call(
        functools.partial(join_kernel, length),
        [sds((length, 3 * inner), BF)] * fan, [vmem()] * 3, mine, others, xz_part,
        flops=fan * length * inner, nbytes=fan * length * inner * 6,
    )
    parts = [parts[0]] + [shift(parts[s], s) for s in range(1, fan)]
    gated, x_raw, x_act = call(
        functools.partial(local_kernel, length, fan, heads),
        [sds((length, inner), BF)] * 3,
        [vmem()] * (fan + 8),
        *parts, packed, bc_act, dtime, x_taps, x_offset, x_past, sinks_x, sinks_b,
        flops=40 * length * inner, nbytes=length * inner * 8,
    )

    gated_all = [gated] + [shift(gated, s) for s in range(1, fan)]
    new_state = call(
        functools.partial(state_kernel, length, heads),
        sds(ssm_state.shape[1:], F32), [smem()] + [vmem()] * 5,
        accepted, packed, dtime, x_act, bc_act, ssm_state[0],
        flops=64 * inner * NS, nbytes=8 * inner * NS,
    )

    cols = out_weight.shape[1]
    out_shape = sds((length, 2 * cols + NS), BF)
    out_parts = call(
        functools.partial(out_kernel, length, fan),
        [out_shape] * fan, [vmem()] * (fan + 2),
        *gated_all, gain, out_pair,
        flops=4 * fan * length * inner * cols, nbytes=4 * inner * cols,
        scratch=[pltpu.VMEM((fan * length, 2 * cols + NS), F32)],
    )

    def to_owner(v, step):
        moves = [
            (f * reqs + j, (j // 2) * reqs + 2 * (f ^ step) + j % 2)
            for f in range(fan)
            for j in range(reqs)
        ]
        return lax.ppermute(v, ("fsdp", "req"), moves)

    arrived = [to_owner(out_parts[s], s) for s in range(fan)]
    mixed = call(
        functools.partial(final_kernel, 2 * cols, inner * fan),
        sds((length, 2 * cols), BF), [vmem()] * fan, *arrived,
        flops=length * cols * 10, nbytes=length * cols * 10,
    )

    def tail_rows(past, fresh):
        joined = jnp.concatenate([past, fresh], axis=0)
        return lax.dynamic_slice_in_dim(joined, accepted[0], KC - 1, 0)[None]

    return (
        mixed[None],
        new_state[None],
        tail_rows(conv_x_state[0], x_raw),
        tail_rows(conv_bc_state[0], bc_raw),
    )


def solution(mesh):
    in_specs = (
        P("req", None, None),
        P("req", "fsdp"),
        P("req", "fsdp"),
        P("req", None),
        P("req", "fsdp"),
        P("fsdp"),
        P("fsdp"),
        P(None, "fsdp"),
        P("fsdp"),
        P(),
        P(),
        P("fsdp"),
        P("fsdp", "req"),
        P("req", None, "fsdp"),
        P("req", None, None),
        P("req", "fsdp", None, None),
        P("req", None, "fsdp"),
        P("req", None, None),
        P("req", None, "fsdp"),
        P("req", None, None),
        P("req", "fsdp", None),
        P("req"),
        P("req"),
        P(),
        P("req"),
        P(),
    )
    out_specs = (
        P("req", None, "fsdp"),
        P("req", "fsdp", None, None),
        P("req", None, "fsdp"),
        P("req", None, None),
    )
    reqs, fan = mesh.shape["req"], mesh.shape["fsdp"]
    assert reqs == 2 * fan and fan & (fan - 1) == 0
    return jax.shard_map(
        functools.partial(per_device, reqs, fan),
        mesh=mesh, in_specs=in_specs, out_specs=out_specs, check_vma=False,
    )
```

```python
import functools

import jax
import jax.numpy as jnp
from jax import lax
from jax.experimental import pallas as pl
from jax.experimental.pallas import tpu as pltpu
from jax.sharding import PartitionSpec as P

HD = 64
NS = 128
KC = 4
EPSILON = 1e-05
BF = jnp.bfloat16
F32 = jnp.float32
VMEM_LIMIT = 20 * 1024 * 1024
BCW = 3 * NS


def vmem():
    return pl.BlockSpec(memory_space=pltpu.VMEM)


def smem():
    return pl.BlockSpec(memory_space=pltpu.SMEM)


def call(body, out_shape, in_specs, *args, flops=0, nbytes=0, scratch=()):
    return pl.pallas_call(
        body,
        out_shape=out_shape,
        in_specs=in_specs,
        out_specs=jax.tree.map(lambda _: vmem(), out_shape),
        scratch_shapes=list(scratch),
        compiler_params=pltpu.CompilerParams(vmem_limit_bytes=VMEM_LIMIT),
        cost_estimate=pl.CostEstimate(flops=flops, bytes_accessed=nbytes, transcendentals=0),
    )(*args)


def hbm():
    return pl.BlockSpec(memory_space=pltpu.HBM)


def in_hbm(v):
    return pltpu.with_memory_space_constraint(v, pltpu.HBM)


def sds(shape, dtype):
    return jax.ShapeDtypeStruct(shape, dtype)


def by_pair(refs):
    return [refs[0]] + list(reversed(refs[1:]))


def silu(v):
    return v / (1.0 + jnp.exp(-v))


def softplus(v):
    return jnp.maximum(v, 0.0) + jnp.log1p(jnp.exp(-jnp.abs(v)))


def conv(history, fresh, taps, offset):
    length = fresh.shape[0]
    joined = jnp.concatenate([history, fresh], axis=0)
    total = offset + taps[0:1] * joined[0:length]
    for k in range(1, KC):
        total = total + taps[k : k + 1] * joined[k : k + length]
    return silu(total)


def running_sum(v):
    length = v.shape[0]
    step = 1
    while step < length:
        v = v + jnp.concatenate([jnp.zeros((step, v.shape[1]), v.dtype), v[: length - step]], axis=0)
        step *= 2
    return v


def head_diag(weights, values):
    heads = len(weights)
    length = weights[0].shape[0]
    if heads == 1:
        return jnp.dot(weights[0], values, preferred_element_type=F32)
    full = jnp.dot(jnp.concatenate(weights, axis=0), values, preferred_element_type=F32)
    owner = lax.broadcasted_iota(jnp.int32, (length, heads * HD), 1) // HD
    out = jnp.where(owner == 0, full[:length], 0.0)
    for i in range(1, heads):
        out = jnp.where(owner == i, full[i * length : (i + 1) * length], out)
    return out


def draft_kernel(fan, share, drafts_hbm, history_hbm, bc_hbm, dt_hbm, x_hbm, z_hbm, out_hbm, *refs):
    lists_hbm, refs = refs[:4], refs[4:]
    outs, lists = refs[:fan], refs[fan + 2 : fan + 6]
    narrow_out, xz_out = refs[fan : fan + 2]
    drafts, history, steps, sems = refs[fan + 6 :]
    half, heads = bc_hbm.shape[0], steps.shape[0]
    copies = [
        pltpu.make_async_copy(source, target, sems.at[i])
        for i, (source, target) in enumerate(
            (
                (drafts_hbm, drafts), (history_hbm, history), (dt_hbm, steps),
                (bc_hbm, narrow_out.at[0:half, 0 : 2 * NS]),
                (x_hbm, xz_out.at[0:half]), (z_hbm, xz_out.at[half : 2 * half]),
                (out_hbm, xz_out.at[2 * half : 3 * half]), *zip(lists_hbm, lists),
            )
        )
    ]
    for c in copies:
        c.start()
    for out in outs:
        out[...] = jnp.zeros_like(out)
    for c in copies[:4]:
        c.wait()
    narrow_out[half : half + heads, :half] = steps[...]
    length = drafts.shape[1]
    pair = lax.axis_index("req") // 2
    past = history[0].astype(F32)
    past = jnp.concatenate([past, jnp.zeros((length - past.shape[0], past.shape[1]), F32)], axis=0)
    if share % 128:
        width = drafts.shape[2]
        whole = drafts[0].astype(F32)
    for s, out in enumerate(outs):
        if share % 128:
            shift = (width - (pair ^ s) * share) % width
            piece = pltpu.roll(whole, shift, 1)[:, :share].astype(BF)
        else:
            start = pl.multiple_of((pair ^ s) * share, 128)
            piece = drafts[0, :, pl.ds(start, share)]
        out[0:length, :share] = piece
        out[length : 2 * length, : 2 * NS] = past.astype(BF)
    for c in copies[4:]:
        c.wait()


def stage_kernel(count, *refs):
    outs, sems = refs[-1 - count : -1], refs[-1]
    copies = [pltpu.make_async_copy(refs[i], outs[i], sems.at[i]) for i in range(count)]
    for c in copies:
        c.start()
    for c in copies:
        c.wait()


def stage(arrays, after):
    return call(
        functools.partial(stage_kernel, len(arrays)),
        [sds(v.shape, v.dtype) for v in arrays],
        [hbm()] * len(arrays) + [pl.BlockSpec(memory_space=pl.ANY)],
        *[in_hbm(v) for v in arrays], after,
        flops=0, nbytes=sum(2 * v.size for v in arrays),
        scratch=[pltpu.SemaphoreType.DMA((len(arrays),))],
    )


def own_and_other(length, half, blocks):
    tokens = jnp.concatenate([b[0:length, : 2 * half] for b in blocks], axis=0)
    first = lax.axis_index("req") % 2 == 0
    low, high = tokens[:, :half], tokens[:, half:]
    return jnp.where(first, low, high), jnp.where(first, high, low)


def project_bc_kernel(length, fan, half, heads, *refs):
    blocks = by_pair(refs[:fan])
    mine, theirs, _, out = refs[fan:]
    own, other = own_and_other(length, half, blocks)
    bc = jnp.dot(own, mine[:half, : 2 * NS], preferred_element_type=F32) + jnp.dot(
        other, theirs[:half, : 2 * NS], preferred_element_type=F32
    )
    turned = (((1,), (1,)), ((), ()))
    rows = slice(half, half + heads)
    dt = lax.dot_general(
        own, mine[rows, :half], turned, preferred_element_type=F32
    ) + lax.dot_general(other, theirs[rows, :half], turned, preferred_element_type=F32)
    dt_hi = dt.astype(BF)
    dt_lo = (dt - dt_hi.astype(F32)).astype(BF)
    out[...] = jnp.concatenate(
        [bc.astype(BF), dt_hi, dt_lo, jnp.zeros((fan * length, NS - 2 * heads), BF)], axis=1
    )


def project_xz_kernel(length, fan, *refs):
    blocks = by_pair(refs[:fan])
    mine, theirs = refs[fan : fan + 2]
    out, out_pair = refs[fan + 2 :]
    half, inner = mine.shape[0] // 3, mine.shape[1]
    own, other = own_and_other(length, half, blocks)
    for i in range(2):
        rows = slice(i * half, (i + 1) * half)
        v = jnp.dot(own, mine[rows], preferred_element_type=F32) + jnp.dot(
            other, theirs[rows], preferred_element_type=F32
        )
        out[:, i * inner : (i + 1) * inner] = v.astype(BF)
    first = lax.axis_index("req") % 2 == 0
    a, b = mine[2 * half :], theirs[2 * half :]
    out_pair[0:half] = jnp.where(first, a, b)
    out_pair[half:] = jnp.where(first, b, a)


def mix_bc_kernel(length, fan, heads, *refs):
    parts = by_pair(refs[:fan])
    blocks = by_pair(refs[fan : 2 * fan])
    taps_ref, offset_ref, bias_ref, rate_ref = refs[2 * fan : 2 * fan + 4]
    packed, bc_raw_o, bc_act_o, dtime_o = refs[2 * fan + 5 :]
    taps, offset = taps_ref[...].astype(F32), offset_ref[...].astype(F32)[None]
    dt_bias, rate = bias_ref[...][None], rate_ref[...][None]
    for t in range(fan):
        acc = None
        for s in range(fan):
            first = length * (t ^ s)
            piece = parts[s][first : first + length].astype(F32)
            acc = piece if acc is None else acc + piece
        bc_raw = acc[:, : 2 * NS].astype(BF)
        dt = acc[:, 2 * NS : 2 * NS + heads] + acc[:, 2 * NS + heads : 2 * NS + 2 * heads]
        history = blocks[t][length : 2 * length, : 2 * NS].astype(F32)[: KC - 1]
        bc_act = conv(history, bc_raw.astype(F32), taps, offset).astype(BF)
        dtime = softplus(dt + dt_bias)
        cumul = running_sum(-rate * dtime)
        packed[t * length : (t + 1) * length, :NS] = bc_act[:, NS:].astype(F32)
        packed[t * length : (t + 1) * length, NS:] = jnp.concatenate(
            [cumul, jnp.zeros((length, NS - heads), F32)], axis=1
        )
        if t == 0:
            bc_raw_o[...] = bc_raw
            bc_act_o[...] = bc_act
            dtime_o[...] = dtime


def is_live(s, slot_req, slot_page, page_count):
    return (slot_req[s] >= 0) & (slot_page[s] < page_count[jnp.maximum(slot_req[s], 0)])


def page_terms(chosen, lists, heads, packed, b_ref, decay_ref, pages, total, order, scores_ref):
    slots, length = scores_ref.shape[:2]
    pair = lax.axis_index("req") // 2
    slot_req, _, _, owner_row = lists

    def rows_of(s):
        row = owner_row[jnp.maximum(slot_req[s], 0)]
        return pl.ds(pl.multiple_of((pair ^ row // 2) * length, length), length)

    for s in range(slots):
        scores_ref[s] = lax.dot_general(
            packed[rows_of(s), :NS].astype(BF), b_ref[s], (((1,), (1,)), ((), ())),
            preferred_element_type=F32,
        )

    def visit(s):
        rows = rows_of(s)
        scores = scores_ref[s]
        cumul = packed[rows, NS:]
        decay = decay_ref[s]
        terms = []
        for first in range(0, heads, 4):
            last = min(first + 4, heads)
            weights = [
                (scores * jnp.exp(cumul[:, h : h + 1] - decay[h : h + 1, :])).astype(BF)
                for h in range(first, last)
            ]
            terms.append(head_diag(weights, pages[s, :, first * HD : last * HD]))
        return rows, terms

    def add(rows, terms):
        first = 0
        for term in terms:
            cols = slice(first, first + term.shape[1])
            total[rows, cols] += term
            first += term.shape[1]

    def two(i, carry):
        one, other = visit(order[2 * i]), visit(order[2 * i + 1])
        add(*one)
        add(*other)
        return carry

    lax.fori_loop(0, chosen // 2, two, 0)

    @pl.when(chosen % 2 == 1)
    def _():
        add(*visit(order[chosen - 1]))


def choose(slots, lists, own, order):
    slot_req, slot_page, page_count, owner_row = lists
    side = lax.axis_index("req") % 2
    count = jnp.int32(0)
    for s in slots:
        row = owner_row[jnp.maximum(slot_req[s], 0)]
        wanted = is_live(s, slot_req, slot_page, page_count) & ((row % 2 == side) == own)

        @pl.when(wanted)
        def _():
            order[count] = s

        count = count + wanted.astype(jnp.int32)
    return count


def fetch_kernel(req, slot, count, x_hbm, _, pages, sems):
    for s in range(x_hbm.shape[0]):
        @pl.when(is_live(s, req, slot, count))
        def _():
            pltpu.make_async_copy(x_hbm.at[s], pages.at[s], sems.at[s]).start()

    for s in range(x_hbm.shape[0]):
        @pl.when(is_live(s, req, slot, count))
        def _():
            pltpu.make_async_copy(x_hbm.at[s], pages.at[s], sems.at[s]).wait()


def first_pages_kernel(
    heads, slot_req, slot_page, page_count, owner_row, packed, b_ref, decay_ref, pages,
    total, order, scores_ref,
):
    lists = (slot_req, slot_page, page_count, owner_row)
    count = choose(range(pages.shape[0] // 2), lists, True, order)
    total[...] = jnp.zeros_like(total)
    page_terms(count, lists, heads, packed, b_ref, decay_ref, pages, total, order, scores_ref)


def other_pages_kernel(
    heads, slot_req, slot_page, page_count, owner_row, packed, b_ref, decay_ref, pages, _,
    out, total, order, scores_ref,
):
    lists = (slot_req, slot_page, page_count, owner_row)
    count = choose(range(pages.shape[0]), lists, False, order)
    total[...] = jnp.zeros_like(total)
    page_terms(count, lists, heads, packed, b_ref, decay_ref, pages, total, order, scores_ref)
    out[...] = total[...].astype(BF)


def last_pages_kernel(
    heads, slot_req, slot_page, page_count, owner_row, packed, b_ref, decay_ref, pages, begun,
    out, total, order, scores_ref,
):
    lists = (slot_req, slot_page, page_count, owner_row)
    slots = pages.shape[0]
    count = choose(range(slots // 2, slots), lists, True, order)
    total[...] = begun[...]
    page_terms(count, lists, heads, packed, b_ref, decay_ref, pages, total, order, scores_ref)
    out[...] = total[...].astype(BF)


def join_kernel(length, mine, other, xz, *outs):
    inner = mine.shape[1]
    for s, out in enumerate(outs):
        rows = slice(s * length, (s + 1) * length)
        out[:, :inner] = (mine[rows].astype(F32) + other[rows].astype(F32)).astype(BF)
        out[:, inner:] = xz[rows]


def local_kernel(length, fan, heads, *refs):
    parts = refs[:fan]
    packed, bc_act, dtime_ref, taps, offset, history, sink_x, sink_b = refs[fan : fan + 8]
    out, x_raw_o, x_act_o = refs[fan + 8 :]
    inner_cols = out.shape[1]
    acc = parts[0][...].astype(F32)
    for s in range(1, fan):
        acc = acc + parts[s][...].astype(F32)
    page_sum = acc[:, :inner_cols]
    x_raw = acc[:, inner_cols : 2 * inner_cols].astype(BF)
    x_raw_o[...] = x_raw
    silu_z = silu(acc[:, 2 * inner_cols :].astype(BF).astype(F32))
    x_act = conv(
        history[0].astype(F32), x_raw.astype(F32), taps[...].astype(F32),
        offset[...].astype(F32)[None],
    ).astype(BF)
    x_act_o[...] = x_act

    c_mat = bc_act[:, NS:]
    b_mat = bc_act[:, :NS]
    turned = (((1,), (1,)), ((), ()))
    inner = lax.dot_general(c_mat, b_mat, turned, preferred_element_type=F32)
    cumul = packed[0:length, NS:]
    dtime = jnp.concatenate(
        [dtime_ref[...], jnp.zeros((length, NS - heads), F32)], axis=1
    )
    cumul_t = jnp.transpose(cumul)
    dtime_t = jnp.transpose(dtime)
    row = lax.broadcasted_iota(jnp.int32, (length, length), 0)
    col = lax.broadcasted_iota(jnp.int32, (length, length), 1)
    later = row >= col
    sink_values = sink_x[0].astype(F32)
    sink_w = lax.dot_general(
        c_mat, sink_b[0], turned, preferred_element_type=F32
    ).astype(BF).astype(F32)
    for first in range(0, heads, 4):
        last = min(first + 4, heads)
        weights = []
        for h in range(first, last):
            spread = jnp.where(later, cumul[:, h : h + 1] - cumul_t[h : h + 1, :], 0.0)
            weights.append(
                jnp.where(later, inner * jnp.exp(spread) * dtime_t[h : h + 1, :], 0.0).astype(BF)
            )
        cols = slice(first * HD, last * HD)
        acc = page_sum[:, cols] + head_diag(weights, x_act[:, cols])
        for q in range(sink_values.shape[0]):
            acc = acc + sink_w[:, q : q + 1] * sink_values[q : q + 1, cols]
        out[:, cols] = (acc * silu_z[:, cols]).astype(BF)


def state_kernel(length, heads, accepted, packed, dtime_ref, x_act, bc_act, ssm, out):
    cumul = packed[0:length, NS : NS + heads]
    count = accepted[0]
    place = lax.broadcasted_iota(jnp.int32, (length, heads), 0)
    last = jnp.sum(jnp.where(place == count - 1, cumul, 0.0), axis=0, keepdims=True)
    kept = place < count
    coeff = jnp.where(kept, jnp.exp(jnp.where(kept, last - cumul, 0.0)) * dtime_ref[...], 0.0)
    factor = jnp.exp(last)
    b_mat = bc_act[:, :NS]
    twice_b = jnp.concatenate([b_mat, b_mat], axis=0)
    for h in range(heads):
        scaled = x_act[:, h * HD : (h + 1) * HD].astype(F32) * coeff[:, h : h + 1]
        high = scaled.astype(BF)
        low = (scaled - high.astype(F32)).astype(BF)
        fresh = lax.dot_general(
            jnp.concatenate([high, low], axis=0), twice_b,
            (((0,), (0,)), ((), ())), preferred_element_type=F32,
        )
        out[h] = factor[:, h : h + 1] * ssm[h] + fresh


def out_kernel(length, fan, *refs):
    blocks = by_pair(refs[:fan])
    gain, weights = refs[fan : fan + 2]
    outs = refs[fan + 2 : 2 * fan + 2]
    whole = refs[2 * fan + 2]
    cols = weights.shape[0]
    me, zed = lax.axis_index("req"), lax.axis_index("fsdp")
    g = jnp.concatenate([b[...] for b in blocks], axis=0).astype(F32)
    squares = jnp.sum(g * g, axis=1, keepdims=True)
    scaled = (g * gain[...].astype(F32)[None]).astype(BF)
    high = squares.astype(BF).astype(F32)
    low = squares - high
    lane = lax.broadcasted_iota(jnp.int32, (fan * length, NS), 1)
    whole[:, :cols] = lax.dot_general(
        scaled, weights[...], (((1,), (1,)), ((), ())), preferred_element_type=F32
    )
    whole[:, cols:] = jnp.where(lane == 0, high, jnp.where(lane == 1, low, 0.0))
    for s, out in enumerate(outs):
        block = me // 2 ^ zed ^ s
        rows = pl.ds(pl.multiple_of(block * length, length), length)
        out[...] = whole[rows, :].astype(BF)


def final_kernel(width, inner_total, *refs):
    parts, out = refs[:-1], refs[-1]
    acc = parts[0][...].astype(F32)
    for p in parts[1:]:
        acc = acc + p[...].astype(F32)
    squares = acc[:, width : width + 1] + acc[:, width + 1 : width + 2]
    out[...] = (acc[:, :width] * lax.rsqrt(squares / inner_total + EPSILON)).astype(BF)


def per_device(
    reqs, fan,
    drafts, x_weight, z_weight, bc_weight, dt_weight, dt_bias, decay_rate,
    conv_x_weight, conv_x_bias, conv_bc_weight, conv_bc_bias, norm_gain, out_weight,
    conv_x_state, conv_bc_state, ssm_state, sink_x, sink_b, page_x, page_b, page_decay,
    slot_req, slot_page, page_count, accepted, owner_row,
):
    _, length, width = drafts.shape
    inner = x_weight.shape[1]
    heads = dt_weight.shape[1]
    slots = page_x.shape[0]

    def swap(v):
        return lax.ppermute(v, "req", [(j, j ^ 1) for j in range(reqs)])

    def shift(v, step):
        return lax.ppermute(v, "req", [(j, j ^ 2 * step) for j in range(reqs)])

    def exchange(own, messages):
        return [own] + [shift(messages[s], s) for s in reversed(range(1, fan))]

    share = width // fan
    wide = max(share, 2 * NS)
    dt_turned = dt_weight.T
    half = x_weight.shape[0]
    places = (slot_req, slot_page, page_count, owner_row)
    packs = call(
        functools.partial(draft_kernel, fan, share),
        [sds((2 * length, wide), BF)] * fan
        + [sds((half + 2 * length, max(2 * NS, -(-half // 128) * 128)), BF), sds((3 * half, inner), BF)]
        + [sds(v.shape, v.dtype) for v in places],
        [hbm()] * 11,
        *[in_hbm(v) for v in (drafts, conv_bc_state, bc_weight, dt_turned, x_weight, z_weight, out_weight.T) + places],
        flops=10, nbytes=2 * length * width,
        scratch=[
            pltpu.VMEM(drafts.shape, BF), pltpu.VMEM(conv_bc_state.shape, BF),
            pltpu.VMEM(dt_turned.shape, BF), pltpu.SemaphoreType.DMA((11,)),
        ],
    )
    blocks, (narrow, xz_weight), lists = packs[:fan], packs[fan : fan + 2], packs[fan + 2 :]
    blocks = exchange(blocks[0], blocks)
    pages = call(
        fetch_kernel, sds(page_x.shape, BF),
        [smem()] * 3 + [hbm(), pl.BlockSpec(memory_space=pl.ANY)],
        *lists[:3], in_hbm(page_x), blocks[3],
        nbytes=2 * page_x.size, scratch=[pltpu.SemaphoreType.DMA((slots,))],
    )
    xz_other = swap(xz_weight)
    bc_cols = 2 * NS + heads
    bc_part = call(
        functools.partial(project_bc_kernel, length, fan, x_weight.shape[0], heads),
        sds((fan * length, BCW), BF), [vmem()] * (fan + 2) + [pl.BlockSpec(memory_space=pl.ANY)],
        *blocks, narrow, swap(narrow), pages,
        flops=2 * fan * length * share * bc_cols, nbytes=2 * share * bc_cols,
    )
    bc_parts = exchange(bc_part, [bc_part] * fan)
    (
        bc_taps, bc_offset, step_bias, rate,
        x_taps, x_offset, gain, x_past, sinks_x, sinks_b, page_b_here, page_decay_here,
    ) = stage(
        (
            conv_bc_weight, conv_bc_bias, dt_bias,
            decay_rate, conv_x_weight, conv_x_bias, norm_gain, conv_x_state, sink_x, sink_b,
            page_b, page_decay,
        ),
        bc_part,
    )
    xz_part, out_pair = call(
        functools.partial(project_xz_kernel, length, fan),
        [sds((fan * length, 2 * inner), BF), sds((2 * half, inner), BF)],
        [vmem()] * (fan + 2),
        *blocks, xz_weight, xz_other,
        flops=4 * fan * length * share * inner, nbytes=4 * share * inner,
    )
    packed, bc_raw, bc_act, dtime = call(
        functools.partial(mix_bc_kernel, length, fan, heads),
        [
            sds((fan * length, 2 * NS), F32),
            sds((length, 2 * NS), BF), sds((length, 2 * NS), BF), sds((length, heads), F32),
        ],
        [vmem()] * (2 * fan + 4) + [pl.BlockSpec(memory_space=pl.ANY)],
        *bc_parts, *blocks, bc_taps, bc_offset, step_bias, rate, xz_part,
        flops=100 * length * NS, nbytes=length * NS * 20,
    )
    packed_other = swap(packed)

    whole = sds((fan * length, inner), F32)
    scratch = [pltpu.SMEM((slots,), jnp.int32), pltpu.VMEM((slots, length, page_x.shape[1]), F32)]
    half_out = sds((fan * length, inner), BF)
    begun = call(
        functools.partial(first_pages_kernel, heads),
        whole, [smem()] * 4 + [vmem()] * 4,
        *lists, packed, page_b_here, page_decay_here, pages,
        flops=2 * slots * length * page_x.shape[1] * inner, nbytes=2 * page_x.size,
        scratch=scratch,
    )
    others = call(
        functools.partial(other_pages_kernel, heads),
        half_out, [smem()] * 4 + [vmem()] * 4 + [pl.BlockSpec(memory_space=pl.ANY)],
        *lists, packed_other, page_b_here, page_decay_here, pages, begun,
        flops=4 * slots * length * page_x.shape[1] * inner, nbytes=2 * page_x.size,
        scratch=[pltpu.VMEM(whole.shape, F32)] + scratch,
    )
    others = swap(others)
    mine = call(
        functools.partial(last_pages_kernel, heads),
        half_out, [smem()] * 4 + [vmem()] * 5,
        *lists, packed, page_b_here, page_decay_here, pages, begun,
        flops=2 * slots * length * page_x.shape[1] * inner, nbytes=2 * page_x.size,
        scratch=[pltpu.VMEM(whole.shape, F32)] + scratch,
    )
    parts = call(
        functools.partial(join_kernel, length),
        [sds((length, 3 * inner), BF)] * fan, [vmem()] * 3, mine, others, xz_part,
        flops=fan * length * inner, nbytes=fan * length * inner * 6,
    )
    parts = exchange(parts[0], parts)
    gated, x_raw, x_act = call(
        functools.partial(local_kernel, length, fan, heads),
        [sds((length, inner), BF)] * 3,
        [vmem()] * (fan + 8),
        *parts, packed, bc_act, dtime, x_taps, x_offset, x_past, sinks_x, sinks_b,
        flops=40 * length * inner, nbytes=length * inner * 8,
    )

    gated_all = exchange(gated, [gated] * fan)
    new_state = call(
        functools.partial(state_kernel, length, heads),
        sds(ssm_state.shape[1:], F32), [smem()] + [vmem()] * 5,
        accepted, packed, dtime, x_act, bc_act, ssm_state[0],
        flops=64 * inner * NS, nbytes=8 * inner * NS,
    )

    cols = out_weight.shape[1]
    out_shape = sds((length, 2 * cols + NS), BF)
    out_parts = call(
        functools.partial(out_kernel, length, fan),
        [out_shape] * fan, [vmem()] * (fan + 2),
        *gated_all, gain, out_pair,
        flops=4 * fan * length * inner * cols, nbytes=4 * inner * cols,
        scratch=[pltpu.VMEM((fan * length, 2 * cols + NS), F32)],
    )

    def to_owner(v, step):
        moves = [
            (f * reqs + j, (j // 2) * reqs + 2 * (f ^ step) + j % 2)
            for f in range(fan)
            for j in range(reqs)
        ]
        return lax.ppermute(v, ("fsdp", "req"), moves)

    arrived = [to_owner(out_parts[s], s) for s in reversed(range(fan))]
    mixed = call(
        functools.partial(final_kernel, 2 * cols, inner * fan),
        sds((length, 2 * cols), BF), [vmem()] * fan, *arrived,
        flops=length * cols * 10, nbytes=length * cols * 10,
    )

    def tail_rows(past, fresh):
        joined = jnp.concatenate([past, fresh], axis=0)
        return lax.dynamic_slice_in_dim(joined, accepted[0], KC - 1, 0)[None]

    return (
        mixed[None],
        new_state[None],
        tail_rows(conv_x_state[0], x_raw),
        tail_rows(conv_bc_state[0], bc_raw),
    )


def solution(mesh):
    in_specs = (
        P("req", None, None),
        P("req", "fsdp"),
        P("req", "fsdp"),
        P("req", None),
        P("req", "fsdp"),
        P("fsdp"),
        P("fsdp"),
        P(None, "fsdp"),
        P("fsdp"),
        P(),
        P(),
        P("fsdp"),
        P("fsdp", "req"),
        P("req", None, "fsdp"),
        P("req", None, None),
        P("req", "fsdp", None, None),
        P("req", None, "fsdp"),
        P("req", None, None),
        P("req", None, "fsdp"),
        P("req", None, None),
        P("req", "fsdp", None),
        P("req"),
        P("req"),
        P(),
        P("req"),
        P(),
    )
    out_specs = (
        P("req", None, "fsdp"),
        P("req", "fsdp", None, None),
        P("req", None, "fsdp"),
        P("req", None, None),
    )
    reqs, fan = mesh.shape["req"], mesh.shape["fsdp"]
    assert reqs == 2 * fan and fan & (fan - 1) == 0
    return jax.shard_map(
        functools.partial(per_device, reqs, fan),
        mesh=mesh, in_specs=in_specs, out_specs=out_specs, check_vma=False,
    )
```

```python
import functools

import jax
import jax.numpy as jnp
from jax import lax
from jax.experimental import pallas as pl
from jax.experimental.pallas import tpu as pltpu
from jax.sharding import PartitionSpec as P

HD = 64
NS = 128
KC = 4
EPSILON = 1e-05
BF = jnp.bfloat16
F32 = jnp.float32
VMEM_LIMIT = 20 * 1024 * 1024
BCW = 3 * NS


def vmem():
    return pl.BlockSpec(memory_space=pltpu.VMEM)


def smem():
    return pl.BlockSpec(memory_space=pltpu.SMEM)


def call(body, out_shape, in_specs, *args, flops=0, nbytes=0, scratch=()):
    return pl.pallas_call(
        body,
        out_shape=out_shape,
        in_specs=in_specs,
        out_specs=jax.tree.map(lambda _: vmem(), out_shape),
        scratch_shapes=list(scratch),
        compiler_params=pltpu.CompilerParams(vmem_limit_bytes=VMEM_LIMIT),
        cost_estimate=pl.CostEstimate(flops=flops, bytes_accessed=nbytes, transcendentals=0),
    )(*args)


def hbm():
    return pl.BlockSpec(memory_space=pltpu.HBM)


def in_hbm(v):
    return pltpu.with_memory_space_constraint(v, pltpu.HBM)


def sds(shape, dtype):
    return jax.ShapeDtypeStruct(shape, dtype)


def by_pair(refs):
    return [refs[0]] + list(reversed(refs[1:]))


def silu(v):
    return v / (1.0 + jnp.exp(-v))


def softplus(v):
    return jnp.maximum(v, 0.0) + jnp.log1p(jnp.exp(-jnp.abs(v)))


def conv(history, fresh, taps, offset):
    length = fresh.shape[0]
    joined = jnp.concatenate([history, fresh], axis=0)
    total = offset + taps[0:1] * joined[0:length]
    for k in range(1, KC):
        total = total + taps[k : k + 1] * joined[k : k + length]
    return silu(total)


def running_sum(v):
    length = v.shape[0]
    step = 1
    while step < length:
        v = v + jnp.concatenate([jnp.zeros((step, v.shape[1]), v.dtype), v[: length - step]], axis=0)
        step *= 2
    return v


def head_diag(weights, values):
    heads = len(weights)
    length = weights[0].shape[0]
    if heads == 1:
        return jnp.dot(weights[0], values, preferred_element_type=F32)
    full = jnp.dot(jnp.concatenate(weights, axis=0), values, preferred_element_type=F32)
    owner = lax.broadcasted_iota(jnp.int32, (length, heads * HD), 1) // HD
    out = jnp.where(owner == 0, full[:length], 0.0)
    for i in range(1, heads):
        out = jnp.where(owner == i, full[i * length : (i + 1) * length], out)
    return out


def draft_kernel(fan, share, drafts_hbm, history_hbm, bc_hbm, dt_hbm, x_hbm, z_hbm, out_hbm, *refs):
    lists_hbm, refs = refs[:4], refs[4:]
    outs, lists = refs[:fan], refs[fan + 2 : fan + 6]
    narrow_out, xz_out = refs[fan : fan + 2]
    drafts, history, steps, sems = refs[fan + 6 :]
    half, heads = bc_hbm.shape[0], steps.shape[0]
    copies = [
        pltpu.make_async_copy(source, target, sems.at[i])
        for i, (source, target) in enumerate(
            (
                (drafts_hbm, drafts), (history_hbm, history), (dt_hbm, steps),
                (bc_hbm, narrow_out.at[0:half, 0 : 2 * NS]),
                (x_hbm, xz_out.at[0:half]), (z_hbm, xz_out.at[half : 2 * half]),
                (out_hbm, xz_out.at[2 * half : 3 * half]), *zip(lists_hbm, lists),
            )
        )
    ]
    for c in copies:
        c.start()
    for out in outs:
        out[...] = jnp.zeros_like(out)
    for c in copies[:4]:
        c.wait()
    narrow_out[half : half + heads, :half] = steps[...]
    length = drafts.shape[1]
    pair = lax.axis_index("req") // 2
    past = history[0].astype(F32)
    past = jnp.concatenate([past, jnp.zeros((length - past.shape[0], past.shape[1]), F32)], axis=0)
    if share % 128:
        width = drafts.shape[2]
        whole = drafts[0].astype(F32)
    for s, out in enumerate(outs):
        if share % 128:
            shift = (width - (pair ^ s) * share) % width
            piece = pltpu.roll(whole, shift, 1)[:, :share].astype(BF)
        else:
            start = pl.multiple_of((pair ^ s) * share, 128)
            piece = drafts[0, :, pl.ds(start, share)]
        out[0:length, :share] = piece
        out[length : 2 * length, : 2 * NS] = past.astype(BF)
    for c in copies[4:]:
        c.wait()


def stage_kernel(count, *refs):
    outs, sems = refs[-1 - count : -1], refs[-1]
    copies = [pltpu.make_async_copy(refs[i], outs[i], sems.at[i]) for i in range(count)]
    for c in copies:
        c.start()
    for c in copies:
        c.wait()


def stage(arrays, after):
    return call(
        functools.partial(stage_kernel, len(arrays)),
        [sds(v.shape, v.dtype) for v in arrays],
        [hbm()] * len(arrays) + [pl.BlockSpec(memory_space=pl.ANY)],
        *[in_hbm(v) for v in arrays], after,
        flops=0, nbytes=sum(2 * v.size for v in arrays),
        scratch=[pltpu.SemaphoreType.DMA((len(arrays),))],
    )


def own_and_other(length, half, blocks):
    tokens = jnp.concatenate([b[0:length, : 2 * half] for b in blocks], axis=0)
    first = lax.axis_index("req") % 2 == 0
    low, high = tokens[:, :half], tokens[:, half:]
    return jnp.where(first, low, high), jnp.where(first, high, low)


def project_bc_kernel(length, fan, half, heads, *refs):
    blocks = by_pair(refs[:fan])
    mine, theirs, _, out = refs[fan:]
    own, other = own_and_other(length, half, blocks)
    bc = jnp.dot(own, mine[:half, : 2 * NS], preferred_element_type=F32) + jnp.dot(
        other, theirs[:half, : 2 * NS], preferred_element_type=F32
    )
    turned = (((1,), (1,)), ((), ()))
    rows = slice(half, half + heads)
    dt = lax.dot_general(
        own, mine[rows, :half], turned, preferred_element_type=F32
    ) + lax.dot_general(other, theirs[rows, :half], turned, preferred_element_type=F32)
    dt_hi = dt.astype(BF)
    dt_lo = (dt - dt_hi.astype(F32)).astype(BF)
    out[...] = jnp.concatenate(
        [bc.astype(BF), dt_hi, dt_lo, jnp.zeros((fan * length, NS - 2 * heads), BF)], axis=1
    )


def project_xz_kernel(length, fan, *refs):
    blocks = by_pair(refs[:fan])
    mine, theirs = refs[fan : fan + 2]
    out, out_pair = refs[fan + 2 :]
    half, inner = mine.shape[0] // 3, mine.shape[1]
    own, other = own_and_other(length, half, blocks)
    for i in range(2):
        rows = slice(i * half, (i + 1) * half)
        v = jnp.dot(own, mine[rows], preferred_element_type=F32) + jnp.dot(
            other, theirs[rows], preferred_element_type=F32
        )
        out[:, i * inner : (i + 1) * inner] = v.astype(BF)
    first = lax.axis_index("req") % 2 == 0
    a, b = mine[2 * half :], theirs[2 * half :]
    out_pair[0:half] = jnp.where(first, a, b)
    out_pair[half:] = jnp.where(first, b, a)


def mix_bc_kernel(length, fan, heads, *refs):
    parts = by_pair(refs[:fan])
    blocks = by_pair(refs[fan : 2 * fan])
    taps_ref, offset_ref, bias_ref, rate_ref = refs[2 * fan : 2 * fan + 4]
    packed, bc_raw_o, bc_act_o, dtime_o = refs[2 * fan + 5 :]
    taps, offset = taps_ref[...].astype(F32), offset_ref[...].astype(F32)[None]
    dt_bias, rate = bias_ref[...][None], rate_ref[...][None]
    for t in range(fan):
        acc = None
        for s in range(fan):
            first = length * (t ^ s)
            piece = parts[s][first : first + length].astype(F32)
            acc = piece if acc is None else acc + piece
        bc_raw = acc[:, : 2 * NS].astype(BF)
        dt = acc[:, 2 * NS : 2 * NS + heads] + acc[:, 2 * NS + heads : 2 * NS + 2 * heads]
        history = blocks[t][length : 2 * length, : 2 * NS].astype(F32)[: KC - 1]
        bc_act = conv(history, bc_raw.astype(F32), taps, offset).astype(BF)
        dtime = softplus(dt + dt_bias)
        cumul = running_sum(-rate * dtime)
        packed[t * length : (t + 1) * length, :NS] = bc_act[:, NS:].astype(F32)
        packed[t * length : (t + 1) * length, NS:] = jnp.concatenate(
            [cumul, jnp.zeros((length, NS - heads), F32)], axis=1
        )
        if t == 0:
            bc_raw_o[...] = bc_raw
            bc_act_o[...] = bc_act
            dtime_o[...] = dtime


def is_live(s, slot_req, slot_page, page_count):
    return (slot_req[s] >= 0) & (slot_page[s] < page_count[jnp.maximum(slot_req[s], 0)])


def page_terms(chosen, length, lists, heads, packed, b_ref, decay_ref, pages, total, order):
    pair = lax.axis_index("req") // 2
    slot_req, _, _, owner_row = lists

    def rows_of(s):
        row = owner_row[jnp.maximum(slot_req[s], 0)]
        return pl.ds(pl.multiple_of((pair ^ row // 2) * length, length), length)

    def visit(s):
        rows = rows_of(s)
        scores = lax.dot_general(
            packed[rows, :NS].astype(BF), b_ref[s], (((1,), (1,)), ((), ())),
            preferred_element_type=F32,
        )
        cumul = packed[rows, NS:]
        decay = decay_ref[s]
        terms = []
        for first in range(0, heads, 4):
            last = min(first + 4, heads)
            weights = [
                (scores * jnp.exp(cumul[:, h : h + 1] - decay[h : h + 1, :])).astype(BF)
                for h in range(first, last)
            ]
            terms.append(head_diag(weights, pages[s, :, first * HD : last * HD]))
        return rows, terms

    def add(rows, terms):
        first = 0
        for term in terms:
            cols = slice(first, first + term.shape[1])
            total[rows, cols] += term
            first += term.shape[1]

    def two(i, carry):
        one, other = visit(order[2 * i]), visit(order[2 * i + 1])
        add(*one)
        add(*other)
        return carry

    lax.fori_loop(0, chosen // 2, two, 0)

    @pl.when(chosen % 2 == 1)
    def _():
        add(*visit(order[chosen - 1]))


def choose(slots, lists, own, order):
    slot_req, slot_page, page_count, owner_row = lists
    side = lax.axis_index("req") % 2
    count = jnp.int32(0)
    for s in slots:
        row = owner_row[jnp.maximum(slot_req[s], 0)]
        wanted = is_live(s, slot_req, slot_page, page_count) & ((row % 2 == side) == own)

        @pl.when(wanted)
        def _():
            order[count] = s

        count = count + wanted.astype(jnp.int32)
    return count


def fetch_kernel(req, slot, count, x_hbm, _, pages, sems):
    for s in range(x_hbm.shape[0]):
        @pl.when(is_live(s, req, slot, count))
        def _():
            pltpu.make_async_copy(x_hbm.at[s], pages.at[s], sems.at[s]).start()

    for s in range(x_hbm.shape[0]):
        @pl.when(is_live(s, req, slot, count))
        def _():
            pltpu.make_async_copy(x_hbm.at[s], pages.at[s], sems.at[s]).wait()


def first_pages_kernel(
    length, heads, slot_req, slot_page, page_count, owner_row, packed, b_ref, decay_ref, pages,
    total, order,
):
    lists = (slot_req, slot_page, page_count, owner_row)
    count = choose(range(pages.shape[0] // 2), lists, True, order)
    total[...] = jnp.zeros_like(total)
    page_terms(count, length, lists, heads, packed, b_ref, decay_ref, pages, total, order)


def other_pages_kernel(
    length, heads, slot_req, slot_page, page_count, owner_row, packed, b_ref, decay_ref, pages, _,
    out, total, order,
):
    lists = (slot_req, slot_page, page_count, owner_row)
    count = choose(range(pages.shape[0]), lists, False, order)
    total[...] = jnp.zeros_like(total)
    page_terms(count, length, lists, heads, packed, b_ref, decay_ref, pages, total, order)
    out[...] = total[...].astype(BF)


def last_pages_kernel(
    length, heads, slot_req, slot_page, page_count, owner_row, packed, b_ref, decay_ref, pages, begun,
    out, total, order,
):
    lists = (slot_req, slot_page, page_count, owner_row)
    slots = pages.shape[0]
    count = choose(range(slots // 2, slots), lists, True, order)
    total[...] = begun[...]
    page_terms(count, length, lists, heads, packed, b_ref, decay_ref, pages, total, order)
    out[...] = total[...].astype(BF)


def join_kernel(length, mine, other, xz, *outs):
    inner = mine.shape[1]
    for s, out in enumerate(outs):
        rows = slice(s * length, (s + 1) * length)
        out[:, :inner] = (mine[rows].astype(F32) + other[rows].astype(F32)).astype(BF)
        out[:, inner:] = xz[rows]


def local_kernel(length, fan, heads, *refs):
    parts = refs[:fan]
    packed, bc_act, dtime_ref, taps, offset, history, sink_x, sink_b = refs[fan : fan + 8]
    out, x_raw_o, x_act_o = refs[fan + 8 :]
    inner_cols = out.shape[1]
    acc = parts[0][...].astype(F32)
    for s in range(1, fan):
        acc = acc + parts[s][...].astype(F32)
    page_sum = acc[:, :inner_cols]
    x_raw = acc[:, inner_cols : 2 * inner_cols].astype(BF)
    x_raw_o[...] = x_raw
    silu_z = silu(acc[:, 2 * inner_cols :].astype(BF).astype(F32))
    x_act = conv(
        history[0].astype(F32), x_raw.astype(F32), taps[...].astype(F32),
        offset[...].astype(F32)[None],
    ).astype(BF)
    x_act_o[...] = x_act

    c_mat = bc_act[:, NS:]
    b_mat = bc_act[:, :NS]
    turned = (((1,), (1,)), ((), ()))
    inner = lax.dot_general(c_mat, b_mat, turned, preferred_element_type=F32)
    cumul = packed[0:length, NS:]
    dtime = jnp.concatenate(
        [dtime_ref[...], jnp.zeros((length, NS - heads), F32)], axis=1
    )
    cumul_t = jnp.transpose(cumul)
    dtime_t = jnp.transpose(dtime)
    row = lax.broadcasted_iota(jnp.int32, (length, length), 0)
    col = lax.broadcasted_iota(jnp.int32, (length, length), 1)
    later = row >= col
    sink_values = sink_x[0].astype(F32)
    sink_w = lax.dot_general(
        c_mat, sink_b[0], turned, preferred_element_type=F32
    ).astype(BF).astype(F32)
    for first in range(0, heads, 4):
        last = min(first + 4, heads)
        weights = []
        for h in range(first, last):
            spread = jnp.where(later, cumul[:, h : h + 1] - cumul_t[h : h + 1, :], 0.0)
            weights.append(
                jnp.where(later, inner * jnp.exp(spread) * dtime_t[h : h + 1, :], 0.0).astype(BF)
            )
        cols = slice(first * HD, last * HD)
        acc = page_sum[:, cols] + head_diag(weights, x_act[:, cols])
        for q in range(sink_values.shape[0]):
            acc = acc + sink_w[:, q : q + 1] * sink_values[q : q + 1, cols]
        out[:, cols] = (acc * silu_z[:, cols]).astype(BF)


def state_kernel(length, heads, accepted, packed, dtime_ref, x_act, bc_act, ssm, out):
    cumul = packed[0:length, NS : NS + heads]
    count = accepted[0]
    place = lax.broadcasted_iota(jnp.int32, (length, heads), 0)
    last = jnp.sum(jnp.where(place == count - 1, cumul, 0.0), axis=0, keepdims=True)
    kept = place < count
    coeff = jnp.where(kept, jnp.exp(jnp.where(kept, last - cumul, 0.0)) * dtime_ref[...], 0.0)
    factor = jnp.exp(last)
    b_mat = bc_act[:, :NS]
    twice_b = jnp.concatenate([b_mat, b_mat], axis=0)
    for h in range(heads):
        scaled = x_act[:, h * HD : (h + 1) * HD].astype(F32) * coeff[:, h : h + 1]
        high = scaled.astype(BF)
        low = (scaled - high.astype(F32)).astype(BF)
        fresh = lax.dot_general(
            jnp.concatenate([high, low], axis=0), twice_b,
            (((0,), (0,)), ((), ())), preferred_element_type=F32,
        )
        out[h] = factor[:, h : h + 1] * ssm[h] + fresh


def out_kernel(length, fan, *refs):
    blocks = by_pair(refs[:fan])
    gain, weights = refs[fan : fan + 2]
    outs = refs[fan + 2 : 2 * fan + 2]
    whole = refs[2 * fan + 2]
    cols = weights.shape[0]
    me, zed = lax.axis_index("req"), lax.axis_index("fsdp")
    g = jnp.concatenate([b[...] for b in blocks], axis=0).astype(F32)
    squares = jnp.sum(g * g, axis=1, keepdims=True)
    scaled = (g * gain[...].astype(F32)[None]).astype(BF)
    high = squares.astype(BF).astype(F32)
    low = squares - high
    lane = lax.broadcasted_iota(jnp.int32, (fan * length, NS), 1)
    whole[:, :cols] = lax.dot_general(
        scaled, weights[...], (((1,), (1,)), ((), ())), preferred_element_type=F32
    )
    whole[:, cols:] = jnp.where(lane == 0, high, jnp.where(lane == 1, low, 0.0))
    for s, out in enumerate(outs):
        block = me // 2 ^ (zed + s) % fan
        rows = pl.ds(pl.multiple_of(block * length, length), length)
        out[...] = whole[rows, :].astype(BF)


def final_kernel(width, inner_total, *refs):
    parts, out = refs[:-1], refs[-1]
    acc = parts[0][...].astype(F32)
    for p in parts[1:]:
        acc = acc + p[...].astype(F32)
    squares = acc[:, width : width + 1] + acc[:, width + 1 : width + 2]
    out[...] = (acc[:, :width] * lax.rsqrt(squares / inner_total + EPSILON)).astype(BF)


def per_device(
    reqs, fan,
    drafts, x_weight, z_weight, bc_weight, dt_weight, dt_bias, decay_rate,
    conv_x_weight, conv_x_bias, conv_bc_weight, conv_bc_bias, norm_gain, out_weight,
    conv_x_state, conv_bc_state, ssm_state, sink_x, sink_b, page_x, page_b, page_decay,
    slot_req, slot_page, page_count, accepted, owner_row,
):
    _, length, width = drafts.shape
    inner = x_weight.shape[1]
    heads = dt_weight.shape[1]
    slots = page_x.shape[0]

    def swap(v):
        return lax.ppermute(v, "req", [(j, j ^ 1) for j in range(reqs)])

    def shift(v, step):
        return lax.ppermute(v, "req", [(j, j ^ 2 * step) for j in range(reqs)])

    def exchange(own, messages):
        return [own] + [shift(messages[s], s) for s in reversed(range(1, fan))]

    share = width // fan
    wide = max(share, 2 * NS)
    dt_turned = dt_weight.T
    half = x_weight.shape[0]
    places = (slot_req, slot_page, page_count, owner_row)
    packs = call(
        functools.partial(draft_kernel, fan, share),
        [sds((2 * length, wide), BF)] * fan
        + [sds((half + 2 * length, max(2 * NS, -(-half // 128) * 128)), BF), sds((3 * half, inner), BF)]
        + [sds(v.shape, v.dtype) for v in places],
        [hbm()] * 11,
        *[in_hbm(v) for v in (drafts, conv_bc_state, bc_weight, dt_turned, x_weight, z_weight, out_weight.T) + places],
        flops=10, nbytes=2 * length * width,
        scratch=[
            pltpu.VMEM(drafts.shape, BF), pltpu.VMEM(conv_bc_state.shape, BF),
            pltpu.VMEM(dt_turned.shape, BF), pltpu.SemaphoreType.DMA((11,)),
        ],
    )
    blocks, (narrow, xz_weight), lists = packs[:fan], packs[fan : fan + 2], packs[fan + 2 :]
    blocks = exchange(blocks[0], blocks)
    pages = call(
        fetch_kernel, sds(page_x.shape, BF),
        [smem()] * 3 + [hbm(), pl.BlockSpec(memory_space=pl.ANY)],
        *lists[:3], in_hbm(page_x), blocks[3],
        nbytes=2 * page_x.size, scratch=[pltpu.SemaphoreType.DMA((slots,))],
    )
    xz_other = swap(xz_weight)
    bc_cols = 2 * NS + heads
    bc_part = call(
        functools.partial(project_bc_kernel, length, fan, x_weight.shape[0], heads),
        sds((fan * length, BCW), BF), [vmem()] * (fan + 2) + [pl.BlockSpec(memory_space=pl.ANY)],
        *blocks, narrow, swap(narrow), pages,
        flops=2 * fan * length * share * bc_cols, nbytes=2 * share * bc_cols,
    )
    bc_parts = exchange(bc_part, [bc_part] * fan)
    (
        bc_taps, bc_offset, step_bias, rate,
        x_taps, x_offset, gain, x_past, sinks_x, sinks_b, page_b_here, page_decay_here,
    ) = stage(
        (
            conv_bc_weight, conv_bc_bias, dt_bias,
            decay_rate, conv_x_weight, conv_x_bias, norm_gain, conv_x_state, sink_x, sink_b,
            page_b, page_decay,
        ),
        bc_part,
    )
    xz_part, out_pair = call(
        functools.partial(project_xz_kernel, length, fan),
        [sds((fan * length, 2 * inner), BF), sds((2 * half, inner), BF)],
        [vmem()] * (fan + 2),
        *blocks, xz_weight, xz_other,
        flops=4 * fan * length * share * inner, nbytes=4 * share * inner,
    )
    packed, bc_raw, bc_act, dtime = call(
        functools.partial(mix_bc_kernel, length, fan, heads),
        [
            sds((fan * length, 2 * NS), F32),
            sds((length, 2 * NS), BF), sds((length, 2 * NS), BF), sds((length, heads), F32),
        ],
        [vmem()] * (2 * fan + 4) + [pl.BlockSpec(memory_space=pl.ANY)],
        *bc_parts, *blocks, bc_taps, bc_offset, step_bias, rate, xz_part,
        flops=100 * length * NS, nbytes=length * NS * 20,
    )
    packed_other = swap(packed)

    whole = sds((fan * length, inner), F32)
    scratch = [pltpu.SMEM((slots,), jnp.int32)]
    half_out = sds((fan * length, inner), BF)
    begun = call(
        functools.partial(first_pages_kernel, length, heads),
        whole, [smem()] * 4 + [vmem()] * 4,
        *lists, packed, page_b_here, page_decay_here, pages,
        flops=2 * slots * length * page_x.shape[1] * inner, nbytes=2 * page_x.size,
        scratch=scratch,
    )
    others = call(
        functools.partial(other_pages_kernel, length, heads),
        half_out, [smem()] * 4 + [vmem()] * 4 + [pl.BlockSpec(memory_space=pl.ANY)],
        *lists, packed_other, page_b_here, page_decay_here, pages, begun,
        flops=4 * slots * length * page_x.shape[1] * inner, nbytes=2 * page_x.size,
        scratch=[pltpu.VMEM(whole.shape, F32)] + scratch,
    )
    others = swap(others)
    mine = call(
        functools.partial(last_pages_kernel, length, heads),
        half_out, [smem()] * 4 + [vmem()] * 5,
        *lists, packed, page_b_here, page_decay_here, pages, begun,
        flops=2 * slots * length * page_x.shape[1] * inner, nbytes=2 * page_x.size,
        scratch=[pltpu.VMEM(whole.shape, F32)] + scratch,
    )
    parts = call(
        functools.partial(join_kernel, length),
        [sds((length, 3 * inner), BF)] * fan, [vmem()] * 3, mine, others, xz_part,
        flops=fan * length * inner, nbytes=fan * length * inner * 6,
    )
    parts = exchange(parts[0], parts)
    gated, x_raw, x_act = call(
        functools.partial(local_kernel, length, fan, heads),
        [sds((length, inner), BF)] * 3,
        [vmem()] * (fan + 8),
        *parts, packed, bc_act, dtime, x_taps, x_offset, x_past, sinks_x, sinks_b,
        flops=40 * length * inner, nbytes=length * inner * 8,
    )

    gated_all = exchange(gated, [gated] * fan)
    new_state = call(
        functools.partial(state_kernel, length, heads),
        sds(ssm_state.shape[1:], F32), [smem()] + [vmem()] * 5,
        accepted, packed, dtime, x_act, bc_act, ssm_state[0],
        flops=64 * inner * NS, nbytes=8 * inner * NS,
    )

    cols = out_weight.shape[1]
    out_shape = sds((length, 2 * cols + NS), BF)
    out_parts = call(
        functools.partial(out_kernel, length, fan),
        [out_shape] * fan, [vmem()] * (fan + 2),
        *gated_all, gain, out_pair,
        flops=4 * fan * length * inner * cols, nbytes=4 * inner * cols,
        scratch=[pltpu.VMEM((fan * length, 2 * cols + NS), F32)],
    )

    def to_owner(v, step):
        moves = [
            (f * reqs + j, (j // 2) * reqs + 2 * ((f + step) % fan) + j % 2)
            for f in range(fan)
            for j in range(reqs)
        ]
        return lax.ppermute(v, ("fsdp", "req"), moves)

    arrived = [to_owner(out_parts[s], s) for s in range(fan)]
    mixed = call(
        functools.partial(final_kernel, 2 * cols, inner * fan),
        sds((length, 2 * cols), BF), [vmem()] * fan, *arrived,
        flops=length * cols * 10, nbytes=length * cols * 10,
    )

    def tail_rows(past, fresh):
        joined = jnp.concatenate([past, fresh], axis=0)
        return lax.dynamic_slice_in_dim(joined, accepted[0], KC - 1, 0)[None]

    return (
        mixed[None],
        new_state[None],
        tail_rows(conv_x_state[0], x_raw),
        tail_rows(conv_bc_state[0], bc_raw),
    )


def solution(mesh):
    in_specs = (
        P("req", None, None),
        P("req", "fsdp"),
        P("req", "fsdp"),
        P("req", None),
        P("req", "fsdp"),
        P("fsdp"),
        P("fsdp"),
        P(None, "fsdp"),
        P("fsdp"),
        P(),
        P(),
        P("fsdp"),
        P("fsdp", "req"),
        P("req", None, "fsdp"),
        P("req", None, None),
        P("req", "fsdp", None, None),
        P("req", None, "fsdp"),
        P("req", None, None),
        P("req", None, "fsdp"),
        P("req", None, None),
        P("req", "fsdp", None),
        P("req"),
        P("req"),
        P(),
        P("req"),
        P(),
    )
    out_specs = (
        P("req", None, "fsdp"),
        P("req", "fsdp", None, None),
        P("req", None, "fsdp"),
        P("req", None, None),
    )
    reqs, fan = mesh.shape["req"], mesh.shape["fsdp"]
    assert reqs == 2 * fan and fan & (fan - 1) == 0
    return jax.shard_map(
        functools.partial(per_device, reqs, fan),
        mesh=mesh, in_specs=in_specs, out_specs=out_specs, check_vma=False,
    )
```
